32 devices in a mesh: dp: 4 (over x, core), enc: 8 (over z, y).
Axes of the slice: x: 2, y: 2, z: 4, core: 2. Of those that a mesh axis runs over, the one named last changes fastest.
Arguments:
- queries: bfloat16 [8, 1024, 768], P('enc', 'dp'), may hold values from -2.5 to 2.5
- passages: bfloat16 [8, 1536, 768], P('enc', 'dp'), may hold values from -0.25 to 0.25
- pattern: int32 [8, 8, 12], P('enc', 'dp'), may hold values 0 or 1
- positive: int32 [8, 8], P('enc', 'dp'), may hold values from 0 to 11
- owners: int32 [8, 48, 1], P('enc', 'dp'), may hold values from 0 to 7; in each aligned block of 12 rows (0 to 11, 12 to 23, ..., all dimensions but the last counted through in order) at most 2 rows name the same one
- encoder_cache: bfloat16 [8, 2048, 768], P('enc', 'dp'), may hold values from -0.75 to 0.75
- proj_weight: bfloat16 [768, 768], replicated, may hold values from -0.21875 to 0.21875
Outputs:
- losses: float32 [8, 1024], P('enc', 'dp')
- question_derivative_lines: bfloat16 [8, 1024, 768], P('enc', 'dp')
- hidden_grad: bfloat16 [8, 2048, 768], P('enc', 'dp')
- weight_grad: float32 [8, 3072, 768], P('enc', 'dp')
The draws below stay inside these ranges and needn't reach their ends.
Inputs may be any that keep to these rules, and one draw needn't show every extreme that they name: `owners`: at most 2 of the 12 spans of one device name the same owner, and some device has exactly 2 for one owner.
All inputs are finite; a program needn't handle non-finite values. No bound on the sum of `pattern` on one device may be relied on, other than what follows from the above.
Results may differ from the reference program's by a relative error of at most 0.0051.
Values may be sent and summed in bfloat16 or wider, within the bound.
A program may use at most 64 MiB of HBM per device.

```python
import math
import jax
import jax.numpy as jnp
import numpy as np
from jax import lax

E = 768
BLOCK = 128
CH = 32
CAP = 2
QB = 2
PB = 3
SPANS = 12
SLOTS = 512
NQB = 8
NPB = 12
N_DP = 4
N_ENC = 8


def positive_blocks(key):
    return jax.random.randint(jax.random.fold_in(key, 303), (N_ENC, N_DP * QB), 0, N_DP * PB, dtype=jnp.int32)


def passage_values(key):
    base_key = jax.random.fold_in(key, 101)
    full_shape = (N_ENC, N_DP * PB * BLOCK, E)
    return 0.036 * jax.random.truncated_normal(base_key, -6.0, 6.0, full_shape, jnp.float32)


def draw_passages(key, part):
    return passage_values(key).astype(jnp.bfloat16)


def draw_positive(key, part):
    return positive_blocks(key)


def draw_queries(key, part):
    base_key = jax.random.fold_in(key, 202)
    full_shape = (N_ENC, N_DP * QB * BLOCK, E)
    scales = jnp.exp(jax.random.uniform(jax.random.fold_in(base_key, 2), (N_ENC, N_DP * QB * BLOCK, 1), jnp.float32, 0.0, math.log(10.0)))
    return (scales * 0.036 * jax.random.truncated_normal(base_key, -6.0, 6.0, full_shape, jnp.float32)).astype(jnp.bfloat16)


def plant(values, stream_key, least, top_value):
    index_at = [jax.random.randint(jax.random.fold_in(stream_key, axis), (), 0, length) for axis, length in enumerate(values.shape)]
    longest = values.shape.index(max(values.shape))
    beside = index_at[:longest] + [(index_at[longest] + 1) % values.shape[longest]] + index_at[longest + 1:]
    return values.at[tuple(index_at)].set(least).at[tuple(beside)].set(top_value)


def levels(key, extent, split, least, high):
    factor_of, own = 1.0, jax.random.fold_in(key, 6)
    for position, shards_of in split:
        draws = jnp.exp(jax.random.uniform(jax.random.fold_in(own, position), (shards_of,), jnp.float32, least / len(split), high / len(split)))
        factor_of = factor_of * jnp.repeat(draws, extent[position] // shards_of).reshape([-1 if axis == position else 1 for axis in range(len(extent))])
    return factor_of


def deal_out(rng, own, number, rows, count, top, most, lean):
    sequence = jax.random.permutation(rng, count)
    packed, ordinary = load_shares(count, rows * top, most, lean, True), load_shares(count, rows * top, most, lean, False)
    places = jnp.arange(count)

    def named(tallies, turn):
        used = int((tallies > 0).sum())
        fixed = max(1, used // 4)
        shifted = fixed + (places - fixed + turn * (used - fixed)) % max(1, count - fixed)
        return jnp.zeros((count,), jnp.int32).at[sequence[jnp.where(places < fixed, places, shifted)]].set(jnp.asarray(tallies, jnp.int32))

    tallies = jnp.where(number % 4 == 0, named(packed, number // 4), named(ordinary, number - number // 4 - 1))
    mixed = jax.random.permutation(jax.random.fold_in(own, 3), count)
    source_of, taker = mixed[0:count // 2 * 2:2], mixed[1:count // 2 * 2:2]
    room = jnp.minimum(tallies[source_of] - 1, most - tallies[taker]) // 2
    room = jnp.where((source_of == sequence[0]) | (taker == sequence[0]) | (tallies[taker] == 0), 0, jnp.maximum(room, 0))
    shifted = jax.random.randint(jax.random.fold_in(own, 4), (count // 2,), 0, 1 << 20) % (room + 1)
    tallies = tallies.at[source_of].add(-shifted).at[taker].add(shifted)
    labels = jnp.searchsorted(jnp.cumsum(tallies), jnp.arange(rows * top), side="right").astype(jnp.int32)
    grid = labels.reshape(top, rows).T
    grid = grid[jax.random.permutation(jax.random.fold_in(own, 1), rows)]
    turn = jax.random.randint(jax.random.fold_in(own, 2), (rows, 1), 0, top)
    return jnp.take_along_axis(grid, (jnp.arange(top)[None, :] + turn) % top, axis=1)


def load_shares(amount, total, reach, skew, full):
    weights = [(1 << 20) // math.isqrt(grade ** skew) + 1 for grade in range(1, amount + 1)]
    largest = reach if full else min(reach, max(-(-total // amount), total * weights[0] // sum(weights)))
    least = 1 if total - largest >= amount - 1 else 0
    counts, surplus = [largest] + [least] * (amount - 1), total - largest - least * (amount - 1)
    while surplus > 0:
        free = [i for i in range(1, amount) if counts[i] < largest] or [i for i in range(1, amount) if counts[i] < reach]
        mass, budget = sum([weights[i] for i in free]), surplus
        for i in free:
            addition = min(reach - counts[i], max(1, budget * weights[i] // mass), surplus)
            counts[i] = counts[i] + addition
            surplus = surplus - addition
    return np.array(counts)


def gaussian(rng, dims, deviation, limit, pieces=(), kind=jnp.bfloat16):
    drawn = deviation * jax.random.normal(rng, dims, jnp.float32)
    if pieces:
        drawn = drawn * levels(rng, dims, pieces, -0.22, 0.18)
    return jnp.clip(drawn, -limit, limit).astype(kind)


def setup_inputs(seed: int = 0) -> dict:
    key_of = jax.random.split(jax.random.key(seed), 8)
    queries = draw_queries(jax.random.fold_in(key_of[7], 71), 0)
    passages = draw_passages(jax.random.fold_in(key_of[7], 71), 0)
    pattern = plant((jax.random.randint(key_of[2], (N_ENC, NQB, NPB), 0, 2) < 1).astype(jnp.int32), jax.random.fold_in(key_of[2], 1), 0, 1)
    positive = draw_positive(jax.random.fold_in(key_of[7], 71), 0)
    owners_keys = jax.random.split(jax.random.fold_in(key_of[4], 1), N_ENC * (N_DP * SPANS) // SPANS)
    owners_turns = jax.random.permutation(jax.random.fold_in(key_of[4], 3), N_ENC * (N_DP * SPANS) // SPANS)
    owners = jax.vmap(lambda own, number: deal_out(jax.random.fold_in(key_of[4], 2), own, number, SPANS, N_ENC, 1, CAP, 2))(owners_keys, owners_turns).reshape((N_ENC, N_DP * SPANS, 1))
    encoder_cache = gaussian(key_of[5], (N_ENC, N_DP * SLOTS, E), 0.05, 0.75, ((0, 8), (1, 4)))
    proj_weight = gaussian(key_of[6], (E, E), E ** -0.5, 0.21875)
    return dict(queries=queries, passages=passages, pattern=pattern, positive=positive, owners=owners, encoder_cache=encoder_cache, proj_weight=proj_weight)


normalizer_coolness_factor = 0.05


def group_terms(inputs):
    question_vector_lines, document_vector_lines, pattern_rows, positive_rows = inputs
    query_count = question_vector_lines.shape[0]
    passage_count = document_vector_lines.shape[0]
    match_energies = jnp.dot(question_vector_lines, document_vector_lines.T, preferred_element_type=jnp.float32) / normalizer_coolness_factor
    block_ids = jnp.arange(passage_count // BLOCK, dtype=jnp.int32)
    allowed_blocks = (pattern_rows == 1) | (block_ids[None, :] == positive_rows[:, None])
    allowed = jnp.repeat(jnp.repeat(allowed_blocks, BLOCK, axis=0), BLOCK, axis=1)
    row_max = jnp.max(jnp.where(allowed, match_energies, -jnp.inf), axis=1, keepdims=True)
    row_sum = jnp.sum(jnp.where(allowed, jnp.exp(match_energies - row_max), 0.0), axis=1)
    log_total = row_max[:, 0] + jnp.log(row_sum)
    row_ids = jnp.arange(query_count, dtype=jnp.int32)
    target = jnp.repeat(positive_rows, BLOCK) * BLOCK + row_ids % BLOCK
    target_hit = target[:, None] == jnp.arange(passage_count, dtype=jnp.int32)[None, :]
    positive_score = jnp.sum(jnp.where(target_hit, match_energies, 0.0), axis=1)
    losses = log_total - positive_score
    probability = jnp.where(allowed, jnp.exp(match_energies - log_total[:, None]), 0.0)
    centered_match_energies = (probability - target_hit.astype(jnp.float32)).astype(jnp.bfloat16)
    question_derivative_lines = (jnp.dot(centered_match_energies, document_vector_lines, preferred_element_type=jnp.float32) / normalizer_coolness_factor).astype(jnp.bfloat16)
    document_derivative_lines = (jnp.dot(centered_match_energies.T, question_vector_lines, preferred_element_type=jnp.float32) / normalizer_coolness_factor).astype(jnp.bfloat16)
    return losses, question_derivative_lines, document_derivative_lines


def route_spans(inputs):
    span_rows, owner_ids = inputs
    owner_hit = (owner_ids[:, None] == jnp.arange(N_ENC, dtype=jnp.int32)[None, :]).astype(jnp.int32)
    earlier = jnp.cumsum(owner_hit, axis=0) - owner_hit
    owner_rank = jnp.sum(earlier * owner_hit, axis=1)
    slot_index = owner_ids * CAP + owner_rank
    selector = (jnp.arange(N_ENC * CAP, dtype=jnp.int32)[:, None] == slot_index[None, :]).astype(jnp.bfloat16)
    return jnp.dot(selector, span_rows, preferred_element_type=jnp.float32).astype(jnp.bfloat16)


def project_back(block_rows, proj_weight):
    return jnp.dot(block_rows, proj_weight.T, preferred_element_type=jnp.float32).astype(jnp.bfloat16)


def cache_product(pair_rows):
    return jnp.dot(pair_rows[0].T, pair_rows[1], preferred_element_type=jnp.float32)


def reference(queries, passages, pattern, positive, owners, encoder_cache, proj_weight):
    losses, question_derivative_lines, document_derivative_lines = lax.map(group_terms, (queries, passages, pattern, positive))
    span_total = PB * BLOCK // CH
    span_rows = document_derivative_lines.reshape(N_ENC * N_DP, span_total, CH * E)
    owner_ids = owners.reshape(N_ENC * N_DP, span_total)
    outgoing = lax.map(route_spans, (span_rows, owner_ids))
    arriving = outgoing.reshape(N_ENC, N_DP, N_ENC, CAP * CH * E).transpose(2, 1, 0, 3)
    arriving = arriving.reshape(N_ENC * N_DP, N_ENC * CAP * CH, E)
    hidden_grad = lax.map(lambda block_rows: project_back(block_rows, proj_weight), arriving)
    caches = encoder_cache.reshape(N_ENC * N_DP, N_ENC * CAP * CH, E)
    weight_grad = lax.map(cache_product, (caches, arriving))
    return (losses, question_derivative_lines, hidden_grad.reshape(N_ENC, N_DP * N_ENC * CAP * CH, E), weight_grad.reshape(N_ENC, N_DP * E, E))
```

```python
import functools

import jax
import jax.numpy as jnp
from jax import lax
from jax.experimental import pallas as pl
from jax.experimental.pallas import tpu as pltpu
from jax.sharding import PartitionSpec as P

BLOCK = 128
CH = 32
CAP = 2
CHUNKS = 4
NEVER = -1e30
INVERSE_COOLNESS = 20.0


def remote(src, dst, send_sem, recv_sem, target):
    return pltpu.make_async_remote_copy(
        src_ref=src,
        dst_ref=dst,
        send_sem=send_sem,
        recv_sem=recv_sem,
        device_id=target,
        device_id_type=pl.DeviceIdType.MESH,
    )


def rows_at(index, count):
    return pl.ds(pl.multiple_of(index * count, count), count)


def group_kernel(
    n_dp, n_enc, q_ref, p_ref, pattern_ref, positive_ref, owners_ref,
    losses_ref, dq_ref, received_ref,
    q_all, p_own, code_out, code_all, s_all, adj, stat_all, dp_sum, outgoing,
    dqs_out, dqs_in, dq_own, dqx_out, dqx_in, select,
    load_sem, qs_sem, qx_send, qx_recv, qf_send, qf_recv, code_send, code_recv,
    stat_send, stat_recv, dqs_send, dqs_recv, dqx_send, dqx_recv, a2a_send, a2a_recv,
):
    me = lax.axis_index("dp")
    my_owner = lax.axis_index("enc")
    n_pair = n_dp // 2
    pair, core = me // 2, me % 2
    sibling = pair * 2 + 1 - core
    rows, width = q_ref.shape
    passage_rows = p_ref.shape[0]
    blocks = passage_rows // BLOCK
    query_blocks = rows // BLOCK
    span_count = passage_rows // CH
    part = rows // CHUNKS
    slot_rows = CAP * CH

    def dp_target(index):
        return {"dp": index}

    barrier = pltpu.get_barrier_semaphore()
    for k in range(1, n_dp):
        pl.semaphore_signal(
            barrier, inc=1, device_id=dp_target((me + k) % n_dp),
            device_id_type=pl.DeviceIdType.MESH,
        )
    for k in range(1, n_enc):
        pl.semaphore_signal(
            barrier, inc=1, device_id={"enc": (my_owner + k) % n_enc},
            device_id_type=pl.DeviceIdType.MESH,
        )
    load_q = pltpu.make_async_copy(q_ref, q_all.at[rows_at(me, rows)], load_sem.at[0])
    load_p = pltpu.make_async_copy(p_ref, p_own, load_sem.at[1])
    load_q.start()
    load_p.start()
    pl.semaphore_wait(barrier, n_dp + n_enc - 2)

    def chunk(source, h):
        return pl.ds(pl.multiple_of(source * rows + h * part, part), part)

    def query_send(t, h):
        target = ((pair + t) % n_pair) * 2 + core
        return remote(
            q_ref.at[pl.ds(h * part, part)], q_all.at[chunk(me, h)],
            qx_send.at[t, h], qx_recv.at[t, h], dp_target(target),
        )

    def query_arrival(t, h):
        source = ((pair - t + n_pair) % n_pair) * 2 + core
        view = q_all.at[chunk(source, h)]
        return remote(view, view, qx_send.at[t, h], qx_recv.at[t, h], dp_target(source))

    def query_forward(t, h, owner_core):
        source = ((pair - t + n_pair) % n_pair) * 2 + owner_core
        view = q_all.at[chunk(source, h)]
        return remote(view, view, qf_send.at[t, h], qf_recv.at[t, h], dp_target(sibling))

    for h in range(CHUNKS):
        for t in range(1, n_pair):
            query_send(t, h).start()
    to_sibling = remote(
        q_ref, q_all.at[rows_at(me, rows)], qs_sem.at[0], qs_sem.at[1], dp_target(sibling)
    )
    to_sibling.start()

    code_out[...] = jnp.zeros_like(code_out)
    for b in range(query_blocks):
        for j in range(n_dp * blocks):
            hit = (positive_ref[0, b] == j).astype(jnp.int32)
            seen = (pattern_ref[0, b, j] == 1).astype(jnp.int32)
            value = jnp.maximum(2 * hit, seen).astype(jnp.float32)
            code_out[j // blocks, j % blocks : j % blocks + 1, b * BLOCK : (b + 1) * BLOCK] = (
                jnp.full((1, BLOCK), value, jnp.float32)
            )
    code_all[me] = code_out[me]

    def code_copy(k):
        target = (me + k) % n_dp
        return remote(
            code_out.at[target], code_all.at[me], code_send.at[k], code_recv.at[k],
            dp_target(target),
        )

    for k in range(1, n_dp):
        code_copy(k).start()

    def select_spans(owner, carry):
        seen = jnp.int32(0)
        found = [jnp.int32(-1)] * CAP
        for c in range(span_count):
            hit = (owners_ref[0, c, 0] == owner).astype(jnp.int32)
            for r in range(CAP):
                found[r] = found[r] + (c + 1) * hit * (seen == r).astype(jnp.int32)
            seen = seen + hit
        line = lax.broadcasted_iota(jnp.int32, (CH, passage_rows), 0)
        column = lax.broadcasted_iota(jnp.int32, (CH, passage_rows), 1)
        for r in range(CAP):
            chosen = (column == line + found[r] * CH).astype(jnp.float32)
            select[rows_at(owner * CAP + r, CH), :] = chosen.astype(jnp.bfloat16)
        return carry

    lax.fori_loop(0, n_enc, select_spans, 0)

    on_diagonal = (
        lax.broadcasted_iota(jnp.int32, (BLOCK, rows), 0)
        == lax.broadcasted_iota(jnp.int32, (BLOCK, rows), 1) % BLOCK
    )

    def score(source):
        columns = rows_at(source, rows)
        scores = lax.dot_general(
            p_own[...], q_all[columns, :], (((1,), (1,)), ((), ())),
            preferred_element_type=jnp.float32,
        ) * INVERSE_COOLNESS
        top = jnp.full((1, rows), NEVER, jnp.float32)
        picked = jnp.zeros((1, rows), jnp.float32)
        masked = []
        for j in range(blocks):
            block = scores[j * BLOCK : (j + 1) * BLOCK, :]
            code = code_all[source, j : j + 1, :]
            block_masked = jnp.where(code > 0.5, block, NEVER)
            s_all[j * BLOCK : (j + 1) * BLOCK, columns] = block_masked
            masked.append(block_masked)
            top = jnp.maximum(top, jnp.max(block_masked, axis=0, keepdims=True))
            hit = on_diagonal & (code > 1.5)
            picked = picked + jnp.sum(jnp.where(hit, block, 0.0), axis=0, keepdims=True)
        shift = jnp.where(top > 0.5 * NEVER, top, 0.0)
        total = jnp.zeros((1, rows), jnp.float32)
        for j in range(blocks):
            total = total + jnp.sum(jnp.exp(masked[j] - shift), axis=0, keepdims=True)
        stat_all[me, 0:1, columns] = jnp.where(
            total > 0.0, shift + jnp.log(jnp.maximum(total, 1e-30)), NEVER
        )
        stat_all[me, 1:2, columns] = picked

    load_q.wait()
    load_p.wait()

    def code_wait(k):
        source = (me - k + n_dp) % n_dp
        remote(
            code_out.at[0], code_all.at[source], code_send.at[k], code_recv.at[k],
            dp_target(source),
        ).wait_recv()

    score(me)
    remote(
        q_ref, q_all.at[rows_at(sibling, rows)], qs_sem.at[0], qs_sem.at[1], dp_target(sibling)
    ).wait_recv()
    for k in range(1, n_dp):
        code_wait(k)
    score(sibling)

    def take_and_forward(t, carry):
        for h in range(CHUNKS):
            query_arrival(t, h).wait_recv()
            query_forward(t, h, core).start()
        score(((pair - t + n_pair) % n_pair) * 2 + core)
        return carry

    lax.fori_loop(1, n_pair, take_and_forward, 0)

    def take_forwarded(t, carry):
        for h in range(CHUNKS):
            query_forward(t, h, 1 - core).wait_recv()
        score(((pair - t + n_pair) % n_pair) * 2 + 1 - core)
        return carry

    lax.fori_loop(1, n_pair, take_forwarded, 0)

    def stat_copy(k, source, target):
        view = stat_all.at[source]
        return remote(view, view, stat_send.at[k], stat_recv.at[k], dp_target(target))

    for k in range(1, n_dp):
        stat_copy(k, me, (me + k) % n_dp).start()
    for k in range(1, n_dp):
        stat_copy(k, (me - k + n_dp) % n_dp, me).wait_recv()

    def adjust(source, carry):
        columns = rows_at(source, rows)
        parts = [stat_all[d, 0:1, columns] for d in range(n_dp)]
        top = functools.reduce(jnp.maximum, parts)
        total = functools.reduce(jnp.add, [jnp.exp(x - top) for x in parts])
        log_total = top + jnp.log(total)
        for j in range(blocks):
            lines = slice(j * BLOCK, (j + 1) * BLOCK)
            hit = on_diagonal & (code_all[source, j : j + 1, :] > 1.5)
            probability = jnp.exp(s_all[lines, columns] - log_total)
            adj[lines, columns] = (probability - jnp.where(hit, 1.0, 0.0)).astype(jnp.bfloat16)
        return carry

    lax.fori_loop(0, n_dp, adjust, 0)

    depth = min(n_dp * rows, 1024)
    if depth == n_dp * rows:
        for n in range(0, width, 256):
            lanes = slice(n, n + 256)
            dp_sum[:, lanes] = jnp.dot(
                adj[...], q_all[:, lanes], preferred_element_type=jnp.float32
            )
    else:
        dp_sum[...] = jnp.zeros_like(dp_sum)

        def add_group(g, carry):
            inner = rows_at(g, depth)
            for n in range(0, width, 256):
                lanes = slice(n, n + 256)
                dp_sum[:, lanes] += jnp.dot(
                    adj[:, inner], q_all[inner, lanes], preferred_element_type=jnp.float32
                )
            return carry

        lax.fori_loop(0, n_dp * rows // depth, add_group, 0)

    for n in range(0, width, 256):
        lanes = slice(n, n + 256)
        grad = (dp_sum[:, lanes] * INVERSE_COOLNESS).astype(jnp.bfloat16)
        outgoing[:, lanes] = jnp.dot(
            select[...], grad, preferred_element_type=jnp.float32
        ).astype(jnp.bfloat16)

    def span_copy(k):
        owner = (my_owner + k) % n_enc
        return remote(
            outgoing.at[rows_at(owner, slot_rows)], received_ref.at[rows_at(my_owner, slot_rows)],
            a2a_send.at[k], a2a_recv.at[k], {"enc": owner},
        )

    def send_spans(k, carry):
        span_copy(k).start()
        return carry

    lax.fori_loop(1, n_enc, send_spans, 0)
    keep = pltpu.make_async_copy(
        outgoing.at[rows_at(my_owner, slot_rows)],
        received_ref.at[rows_at(my_owner, slot_rows)],
        load_sem.at[2],
    )
    keep.start()

    def partial(source):
        return lax.dot_general(
            adj[:, rows_at(source, rows)], p_own[...], (((0,), (0,)), ((), ())),
            preferred_element_type=jnp.float32,
        )

    def dqs_copy(t):
        return remote(
            dqs_out.at[t], dqs_in.at[t], dqs_send.at[t], dqs_recv.at[t], dp_target(sibling)
        )

    def dqx_copy(t):
        target = ((pair + t) % n_pair) * 2 + core
        return remote(
            dqx_out.at[t], dqx_in.at[t], dqx_send.at[t], dqx_recv.at[t], dp_target(target)
        )

    def sibling_share(t, carry):
        target = ((pair + t) % n_pair) * 2
        dqs_out[t] = partial(target + 1 - core).astype(jnp.bfloat16)
        dqs_copy(t).start()
        return carry

    def chip_share(t, carry):
        target = ((pair + t) % n_pair) * 2
        dq_own[...] = partial(target + core)
        dqs_copy(t).wait_recv()
        dqx_out[t] = (dq_own[...] + dqs_in[t].astype(jnp.float32)).astype(jnp.bfloat16)
        dqx_copy(t).start()
        return carry

    lax.fori_loop(1, n_pair, sibling_share, 0)
    lax.fori_loop(1, n_pair, chip_share, 0)
    sibling_share(0, 0)
    dq_own[...] = partial(me)
    dqs_copy(0).wait_recv()
    dq_own[...] += dqs_in[0].astype(jnp.float32)

    own = rows_at(me, rows)
    parts = [stat_all[d, 0:1, own] for d in range(n_dp)]
    top = functools.reduce(jnp.maximum, parts)
    total = functools.reduce(jnp.add, [jnp.exp(x - top) for x in parts])
    picked = functools.reduce(jnp.add, [stat_all[d, 1:2, own] for d in range(n_dp)])
    losses_ref[...] = top + jnp.log(total) - picked

    def add_chip(t, carry):
        dqx_copy(t).wait_recv()
        dq_own[...] += dqx_in[t].astype(jnp.float32)
        return carry

    lax.fori_loop(1, n_pair, add_chip, 0)
    dq_ref[...] = (dq_own[...] * INVERSE_COOLNESS).astype(jnp.bfloat16)

    to_sibling.wait_send()
    for t in range(1, n_pair):
        for h in range(CHUNKS):
            query_send(t, h).wait_send()
            query_forward(t, h, core).wait_send()
    for k in range(1, n_dp):
        code_copy(k).wait_send()
        stat_copy(k, me, (me + k) % n_dp).wait_send()
    for t in range(n_pair):
        dqs_copy(t).wait_send()
        if t:
            dqx_copy(t).wait_send()
    for k in range(1, n_enc):
        span_copy(k).wait_send()
    for k in range(1, n_enc):
        source = (my_owner - k + n_enc) % n_enc
        remote(
            outgoing.at[rows_at(source, slot_rows)], received_ref.at[rows_at(source, slot_rows)],
            a2a_send.at[k], a2a_recv.at[k], {"enc": source},
        ).wait_recv()
    keep.wait()


def body(n_dp, n_enc, queries, passages, pattern, positive, owners, encoder_cache, proj_weight):
    rows, width = queries.shape[1:]
    passage_rows = passages.shape[1]
    blocks = passage_rows // BLOCK
    code_rows = -(-blocks // 8) * 8
    n_pair = n_dp // 2
    total_rows = n_dp * rows
    slots = n_enc * CAP * CH
    bf16, f32 = jnp.bfloat16, jnp.float32
    dma = pltpu.SemaphoreType.DMA
    smem = pl.BlockSpec(memory_space=pltpu.SMEM)
    vmem = pl.BlockSpec(memory_space=pltpu.VMEM)
    hbm = pl.BlockSpec(memory_space=pl.ANY)
    losses, dq, received = pl.pallas_call(
        functools.partial(group_kernel, n_dp, n_enc),
        out_shape=(
            jax.ShapeDtypeStruct((1, rows), f32),
            jax.ShapeDtypeStruct((rows, width), bf16),
            jax.ShapeDtypeStruct((slots, width), bf16),
        ),
        in_specs=[hbm, hbm, smem, smem, smem],
        out_specs=(vmem, vmem, hbm),
        scratch_shapes=[
            pltpu.VMEM((total_rows, width), bf16),
            pltpu.VMEM((passage_rows, width), bf16),
            pltpu.VMEM((n_dp, code_rows, rows), f32),
            pltpu.VMEM((n_dp, code_rows, rows), f32),
            pltpu.VMEM((passage_rows, total_rows), f32),
            pltpu.VMEM((passage_rows, total_rows), bf16),
            pltpu.VMEM((n_dp, 2, total_rows), f32),
            pltpu.VMEM((passage_rows, width), f32),
            pltpu.VMEM((slots, width), bf16),
            pltpu.VMEM((n_pair, rows, width), bf16),
            pltpu.VMEM((n_pair, rows, width), bf16),
            pltpu.VMEM((rows, width), f32),
            pltpu.VMEM((n_pair, rows, width), bf16),
            pltpu.VMEM((n_pair, rows, width), bf16),
            pltpu.VMEM((slots, passage_rows), bf16),
            dma((3,)),
            dma((2,)),
            dma((n_pair, CHUNKS)),
            dma((n_pair, CHUNKS)),
            dma((n_pair, CHUNKS)),
            dma((n_pair, CHUNKS)),
            dma((n_dp,)),
            dma((n_dp,)),
            dma((n_dp,)),
            dma((n_dp,)),
            dma((n_pair,)),
            dma((n_pair,)),
            dma((n_pair,)),
            dma((n_pair,)),
            dma((n_enc,)),
            dma((n_enc,)),
        ],
        compiler_params=pltpu.CompilerParams(
            collective_id=0, has_side_effects=True, vmem_limit_bytes=56 * 1024 * 1024
        ),
        cost_estimate=pl.CostEstimate(
            flops=6 * total_rows * passage_rows * width,
            bytes_accessed=4 * slots * width,
            transcendentals=2 * total_rows * passage_rows,
        ),
    )(queries[0], passages[0], pattern, positive, owners)
    hidden_grad = jnp.dot(received, proj_weight.T, preferred_element_type=f32).astype(bf16)
    weight_grad = jnp.dot(encoder_cache[0].T, received, preferred_element_type=f32)
    return (losses, dq[None], hidden_grad[None], weight_grad[None])


def solution(mesh):
    placed = (
        P("enc", "dp", None),
        P("enc", "dp", None),
        P("enc", "dp", None),
        P("enc", "dp"),
        P("enc", "dp", None),
        P("enc", "dp", None),
        P(),
    )
    return jax.shard_map(
        functools.partial(body, mesh.shape["dp"], mesh.shape["enc"]),
        mesh=mesh,
        in_specs=placed,
        out_specs=(
            P("enc", "dp"),
            P("enc", "dp", None),
            P("enc", "dp", None),
            P("enc", "dp", None),
        ),
        check_vma=False,
    )
```

```python
import functools

import jax
import jax.numpy as jnp
from jax import lax
from jax.experimental import pallas as pl
from jax.experimental.pallas import tpu as pltpu
from jax.sharding import PartitionSpec as P

BLOCK = 128
CH = 32
CAP = 2
CHUNKS = 4
LANES = 256
NEVER = -1e30
INVERSE_COOLNESS = 20.0


def remote(src, dst, send_sem, recv_sem, target):
    return pltpu.make_async_remote_copy(
        src_ref=src,
        dst_ref=dst,
        send_sem=send_sem,
        recv_sem=recv_sem,
        device_id=target,
        device_id_type=pl.DeviceIdType.MESH,
    )


def rows_at(index, count):
    return pl.ds(pl.multiple_of(index * count, count), count)


def group_kernel(
    n_dp, n_enc, q_ref, p_ref, pattern_ref, positive_ref, owners_ref,
    losses_ref, dq_ref, received_ref,
    q_all, p_own, code_out, code_all, e_all, adj, stat_all, dp_sum, outgoing,
    dqs_out, dqs_in, dq_own, dqx_out, dqx_in, select, top_all,
    load_sem, qs_sem, qx_send, qx_recv, qf_send, qf_recv, code_send, code_recv,
    stat_send, stat_recv, dqs_send, dqs_recv, dqx_send, dqx_recv, a2a_send, a2a_recv,
):
    me = lax.axis_index("dp")
    my_owner = lax.axis_index("enc")
    n_pair = n_dp // 2
    pair, core = me // 2, me % 2
    sibling = pair * 2 + 1 - core
    rows, width = q_ref.shape
    passage_rows = p_ref.shape[0]
    blocks = passage_rows // BLOCK
    query_blocks = rows // BLOCK
    span_count = passage_rows // CH
    part = rows // CHUNKS
    slot_rows = CAP * CH

    def dp_target(index):
        return {"dp": index}

    barrier = pltpu.get_barrier_semaphore()
    for k in range(1, n_dp):
        pl.semaphore_signal(
            barrier, inc=1, device_id=dp_target((me + k) % n_dp),
            device_id_type=pl.DeviceIdType.MESH,
        )
    for k in range(1, n_enc):
        pl.semaphore_signal(
            barrier, inc=1, device_id={"enc": (my_owner + k) % n_enc},
            device_id_type=pl.DeviceIdType.MESH,
        )
    load_q = pltpu.make_async_copy(q_ref, q_all.at[rows_at(me, rows)], load_sem.at[0])
    load_p = pltpu.make_async_copy(p_ref, p_own, load_sem.at[1])
    load_q.start()
    load_p.start()
    pl.semaphore_wait(barrier, n_dp + n_enc - 2)

    def chunk(source, h):
        return pl.ds(pl.multiple_of(source * rows + h * part, part), part)

    def query_send(t, h):
        target = ((pair + t) % n_pair) * 2 + core
        return remote(
            q_ref.at[pl.ds(h * part, part)], q_all.at[chunk(me, h)],
            qx_send.at[t, h], qx_recv.at[t, h], dp_target(target),
        )

    def query_arrival(t, h):
        source = ((pair - t + n_pair) % n_pair) * 2 + core
        view = q_all.at[chunk(source, h)]
        return remote(view, view, qx_send.at[t, h], qx_recv.at[t, h], dp_target(source))

    def query_forward(t, h, owner_core):
        source = ((pair - t + n_pair) % n_pair) * 2 + owner_core
        view = q_all.at[chunk(source, h)]
        return remote(view, view, qf_send.at[t, h], qf_recv.at[t, h], dp_target(sibling))

    for h in range(CHUNKS):
        for t in range(1, n_pair):
            query_send(t, h).start()
    to_sibling = remote(
        q_ref, q_all.at[rows_at(me, rows)], qs_sem.at[0], qs_sem.at[1], dp_target(sibling)
    )
    to_sibling.start()

    code_out[...] = jnp.zeros_like(code_out)
    for b in range(query_blocks):
        for j in range(n_dp * blocks):
            hit = (positive_ref[0, b] == j).astype(jnp.int32)
            seen = (pattern_ref[0, b, j] == 1).astype(jnp.int32)
            value = jnp.maximum(2 * hit, seen).astype(jnp.float32)
            code_out[j // blocks, j % blocks : j % blocks + 1, b * BLOCK : (b + 1) * BLOCK] = (
                jnp.full((1, BLOCK), value, jnp.float32)
            )
    code_all[me] = code_out[me]

    def code_copy(k):
        target = (me + k) % n_dp
        return remote(
            code_out.at[target], code_all.at[me], code_send.at[k], code_recv.at[k],
            dp_target(target),
        )

    for k in range(1, n_dp):
        code_copy(k).start()

    def select_spans(owner, carry):
        seen = jnp.int32(0)
        found = [jnp.int32(-1)] * CAP
        for c in range(span_count):
            hit = (owners_ref[0, 0, c] == owner).astype(jnp.int32)
            for r in range(CAP):
                found[r] = found[r] + (c + 1) * hit * (seen == r).astype(jnp.int32)
            seen = seen + hit
        line = lax.broadcasted_iota(jnp.int32, (CH, passage_rows), 0)
        column = lax.broadcasted_iota(jnp.int32, (CH, passage_rows), 1)
        for r in range(CAP):
            chosen = (column == line + found[r] * CH).astype(jnp.float32)
            select[rows_at(owner * CAP + r, CH), :] = chosen.astype(jnp.bfloat16)
        return carry

    lax.fori_loop(0, n_enc, select_spans, 0)

    on_diagonal = lax.broadcasted_iota(jnp.int32, (BLOCK, BLOCK), 0) == lax.broadcasted_iota(
        jnp.int32, (BLOCK, BLOCK), 1
    )

    def score(source, b):
        columns = pl.ds(pl.multiple_of(source * rows + b * BLOCK, BLOCK), BLOCK)
        inner = pl.ds(b * BLOCK, BLOCK)
        scores = lax.dot_general(
            p_own[...], q_all[columns, :], (((1,), (1,)), ((), ())),
            preferred_element_type=jnp.float32,
        ) * INVERSE_COOLNESS
        top = jnp.full((1, BLOCK), NEVER, jnp.float32)
        picked = jnp.zeros((1, BLOCK), jnp.float32)
        masked = []
        for j in range(blocks):
            block = scores[j * BLOCK : (j + 1) * BLOCK, :]
            code = code_all[source, j : j + 1, inner]
            block_masked = jnp.where(code > 0.5, block, NEVER)
            masked.append(block_masked)
            top = jnp.maximum(top, jnp.max(block_masked, axis=0, keepdims=True))
            hit = on_diagonal & (code > 1.5)
            picked = picked + jnp.sum(jnp.where(hit, block, 0.0), axis=0, keepdims=True)
        shift = jnp.where(top > 0.5 * NEVER, top, 0.0)
        total = jnp.zeros((1, BLOCK), jnp.float32)
        for j in range(blocks):
            terms = jnp.exp(masked[j] - shift)
            e_all[j * BLOCK : (j + 1) * BLOCK, columns] = terms
            total = total + jnp.sum(terms, axis=0, keepdims=True)
        top_all[0:1, columns] = top
        stat_all[me, 0:1, columns] = jnp.where(
            total > 0.0, shift + jnp.log(jnp.maximum(total, 1e-30)), NEVER
        )
        stat_all[me, 1:2, columns] = picked

    load_q.wait()
    load_p.wait()

    def code_wait(k):
        source = (me - k + n_dp) % n_dp
        remote(
            code_out.at[0], code_all.at[source], code_send.at[k], code_recv.at[k],
            dp_target(source),
        ).wait_recv()

    for b in range(query_blocks):
        score(me, b)
    remote(
        q_ref, q_all.at[rows_at(sibling, rows)], qs_sem.at[0], qs_sem.at[1], dp_target(sibling)
    ).wait_recv()
    for k in range(1, n_dp):
        code_wait(k)
    for b in range(query_blocks):
        score(sibling, b)

    per_block = CHUNKS // query_blocks

    def take(t, carry):
        first = ((pair - t + n_pair) % n_pair) * 2
        for b in range(query_blocks):
            for h in range(b * per_block, (b + 1) * per_block):
                query_arrival(t, h).wait_recv()
                query_forward(t, h, core).start()
            score(first + core, b)
            for h in range(b * per_block, (b + 1) * per_block):
                query_forward(t, h, 1 - core).wait_recv()
            score(first + 1 - core, b)
        return carry

    lax.fori_loop(1, n_pair, take, 0)

    def stat_copy(k, source, target):
        view = stat_all.at[source]
        return remote(view, view, stat_send.at[k], stat_recv.at[k], dp_target(target))

    for k in range(1, n_dp):
        stat_copy(k, me, (me + k) % n_dp).start()
    for k in range(1, n_dp):
        stat_copy(k, (me - k + n_dp) % n_dp, me).wait_recv()

    def adjust(source, carry):
        columns = rows_at(source, rows)
        parts = [stat_all[d, 0:1, columns] for d in range(n_dp)]
        top = functools.reduce(jnp.maximum, parts)
        total = functools.reduce(jnp.add, [jnp.exp(x - top) for x in parts])
        log_total = top + jnp.log(total)
        factor = jnp.exp(top_all[0:1, columns] - log_total)
        hit_rows = jnp.concatenate([on_diagonal] * query_blocks, axis=1)
        for j in range(blocks):
            lines = slice(j * BLOCK, (j + 1) * BLOCK)
            hit = hit_rows & (code_all[source, j : j + 1, :] > 1.5)
            probability = e_all[lines, columns] * factor
            adj[lines, columns] = (probability - jnp.where(hit, 1.0, 0.0)).astype(jnp.bfloat16)
        return carry

    lax.fori_loop(0, n_dp, adjust, 0)

    half = n_enc // 2
    my_half, my_place = my_owner // half, my_owner % half
    tiles = width // LANES

    def to_owner(j, across):
        side = (1 - my_half) if across else my_half
        return side * half + (my_place + j) % half

    def from_owner(j, across):
        side = (1 - my_half) if across else my_half
        return side * half + (my_place - j + half) % half

    def span_copy(j, across, n, owner, place):
        lanes = pl.ds(n * LANES, LANES)
        sem = j + (0 if across else half)
        return remote(
            outgoing.at[rows_at(owner, slot_rows), lanes],
            received_ref.at[rows_at(place, slot_rows), lanes],
            a2a_send.at[sem, n], a2a_recv.at[sem, n], {"enc": owner},
        )

    depth = min(n_dp * rows, 1024)
    for n in range(tiles):
        lanes = slice(n * LANES, (n + 1) * LANES)
        if depth == n_dp * rows:
            total = jnp.dot(adj[...], q_all[:, lanes], preferred_element_type=jnp.float32)
        else:
            dp_sum[...] = jnp.zeros_like(dp_sum)

            def add_group(g, carry, lanes=lanes):
                inner = rows_at(g, depth)
                dp_sum[...] += jnp.dot(
                    adj[:, inner], q_all[inner, lanes], preferred_element_type=jnp.float32
                )
                return carry

            lax.fori_loop(0, n_dp * rows // depth, add_group, 0)
            total = dp_sum[...]
        grad = (total * INVERSE_COOLNESS).astype(jnp.bfloat16)
        outgoing[:, lanes] = jnp.dot(
            select[...], grad, preferred_element_type=jnp.float32
        ).astype(jnp.bfloat16)
        for j in range(half):
            span_copy(j, True, n, to_owner(j, True), my_owner).start()
            if j:
                span_copy(j, False, n, to_owner(j, False), my_owner).start()

    keep = pltpu.make_async_copy(
        outgoing.at[rows_at(my_owner, slot_rows)],
        received_ref.at[rows_at(my_owner, slot_rows)],
        load_sem.at[2],
    )
    keep.start()

    def partial(source):
        return lax.dot_general(
            adj[:, rows_at(source, rows)], p_own[...], (((0,), (0,)), ((), ())),
            preferred_element_type=jnp.float32,
        )

    def dqs_copy(t):
        return remote(
            dqs_out.at[t], dqs_in.at[t], dqs_send.at[t], dqs_recv.at[t], dp_target(sibling)
        )

    def dqx_copy(t):
        target = ((pair + t) % n_pair) * 2 + core
        return remote(
            dqx_out.at[t], dqx_in.at[t], dqx_send.at[t], dqx_recv.at[t], dp_target(target)
        )

    def sibling_share(t, carry):
        target = ((pair + t) % n_pair) * 2
        dqs_out[t] = partial(target + 1 - core).astype(jnp.bfloat16)
        dqs_copy(t).start()
        return carry

    def chip_share(t, carry):
        target = ((pair + t) % n_pair) * 2
        dq_own[...] = partial(target + core)
        dqs_copy(t).wait_recv()
        dqx_out[t] = (dq_own[...] + dqs_in[t].astype(jnp.float32)).astype(jnp.bfloat16)
        dqx_copy(t).start()
        return carry

    lax.fori_loop(1, n_pair, sibling_share, 0)
    lax.fori_loop(1, n_pair, chip_share, 0)
    sibling_share(0, 0)
    dq_own[...] = partial(me)
    dqs_copy(0).wait_recv()
    dq_own[...] += dqs_in[0].astype(jnp.float32)

    own = rows_at(me, rows)
    parts = [stat_all[d, 0:1, own] for d in range(n_dp)]
    top = functools.reduce(jnp.maximum, parts)
    total = functools.reduce(jnp.add, [jnp.exp(x - top) for x in parts])
    picked = functools.reduce(jnp.add, [stat_all[d, 1:2, own] for d in range(n_dp)])
    losses_ref[...] = top + jnp.log(total) - picked

    def add_chip(t, carry):
        dqx_copy(t).wait_recv()
        dq_own[...] += dqx_in[t].astype(jnp.float32)
        return carry

    lax.fori_loop(1, n_pair, add_chip, 0)
    dq_ref[...] = (dq_own[...] * INVERSE_COOLNESS).astype(jnp.bfloat16)

    to_sibling.wait_send()
    for t in range(1, n_pair):
        for h in range(CHUNKS):
            query_send(t, h).wait_send()
            query_forward(t, h, core).wait_send()
    for k in range(1, n_dp):
        code_copy(k).wait_send()
        stat_copy(k, me, (me + k) % n_dp).wait_send()
    for t in range(n_pair):
        dqs_copy(t).wait_send()
        if t:
            dqx_copy(t).wait_send()
    for n in range(tiles):
        for j in range(half):
            for across in (True, False) if j else (True,):
                span_copy(j, across, n, to_owner(j, across), my_owner).wait_send()
                source = from_owner(j, across)
                span_copy(j, across, n, source, source).wait_recv()
    keep.wait()


def owner_kernel(
    received_ref, cache_ref, weight_ref, losses_in, dq_in,
    hidden_ref, grad_ref, losses_ref, dq_ref,
    received, cache, weight, hidden, grad, in_sem, out_sem,
):
    loads = [
        pltpu.make_async_copy(source, place, in_sem.at[i])
        for i, (source, place) in enumerate(
            [
                (received_ref, received),
                (cache_ref, cache),
                (weight_ref, weight),
                (dq_in, dq_ref),
                (losses_in, losses_ref),
            ]
        )
    ]
    for load in loads:
        load.start()
    loads[0].wait()
    loads[1].wait()
    stores = []

    def store(source, place, lines):
        copy = pltpu.make_async_copy(
            source.at[lines], place.at[lines], out_sem.at[len(stores)]
        )
        copy.start()
        stores.append(copy)

    for n in range(0, cache.shape[1], LANES):
        lines = pl.ds(n, LANES)
        grad[lines, :] = lax.dot_general(
            cache[:, lines], received[...], (((0,), (0,)), ((), ())),
            preferred_element_type=jnp.float32,
        )
        store(grad, grad_ref, lines)
    loads[2].wait()
    part = received.shape[0] // 2
    for n in range(2):
        lines = pl.ds(n * part, part)
        hidden[lines, :] = lax.dot_general(
            received[lines, :], weight[...], (((1,), (1,)), ((), ())),
            preferred_element_type=jnp.float32,
        ).astype(jnp.bfloat16)
        store(hidden, hidden_ref, lines)
    loads[3].wait()
    loads[4].wait()
    for copy in stores:
        copy.wait()


def body(n_dp, n_enc, queries, passages, pattern, positive, owners, encoder_cache, proj_weight):
    rows, width = queries.shape[1:]
    passage_rows = passages.shape[1]
    blocks = passage_rows // BLOCK
    code_rows = -(-blocks // 4) * 4
    n_pair = n_dp // 2
    total_rows = n_dp * rows
    slots = n_enc * CAP * CH
    bf16, f32 = jnp.bfloat16, jnp.float32
    dma = pltpu.SemaphoreType.DMA
    smem = pl.BlockSpec(memory_space=pltpu.SMEM)
    vmem = pl.BlockSpec(memory_space=pltpu.VMEM)
    hbm = pl.BlockSpec(memory_space=pl.ANY)
    losses, dq, received = pl.pallas_call(
        functools.partial(group_kernel, n_dp, n_enc),
        out_shape=(
            jax.ShapeDtypeStruct((1, rows), f32),
            jax.ShapeDtypeStruct((rows, width), bf16),
            jax.ShapeDtypeStruct((slots, width), bf16),
        ),
        in_specs=[hbm, hbm, smem, smem, smem],
        out_specs=(vmem, vmem, hbm),
        scratch_shapes=[
            pltpu.VMEM((total_rows, width), bf16),
            pltpu.VMEM((passage_rows, width), bf16),
            pltpu.VMEM((n_dp, code_rows, rows), f32),
            pltpu.VMEM((n_dp, code_rows, rows), f32),
            pltpu.VMEM((passage_rows, total_rows), f32),
            pltpu.VMEM((passage_rows, total_rows), bf16),
            pltpu.VMEM((n_dp, 2, total_rows), f32),
            pltpu.VMEM((passage_rows, LANES), f32),
            pltpu.VMEM((slots, width), bf16),
            pltpu.VMEM((n_pair, rows, width), bf16),
            pltpu.VMEM((n_pair, rows, width), bf16),
            pltpu.VMEM((rows, width), f32),
            pltpu.VMEM((n_pair, rows, width), bf16),
            pltpu.VMEM((n_pair, rows, width), bf16),
            pltpu.VMEM((slots, passage_rows), bf16),
            pltpu.VMEM((1, total_rows), f32),
            dma((3,)),
            dma((2,)),
            dma((n_pair, CHUNKS)),
            dma((n_pair, CHUNKS)),
            dma((n_pair, CHUNKS)),
            dma((n_pair, CHUNKS)),
            dma((n_dp,)),
            dma((n_dp,)),
            dma((n_dp,)),
            dma((n_dp,)),
            dma((n_pair,)),
            dma((n_pair,)),
            dma((n_pair,)),
            dma((n_pair,)),
            dma((n_enc, width // LANES)),
            dma((n_enc, width // LANES)),
        ],
        compiler_params=pltpu.CompilerParams(
            collective_id=0, has_side_effects=True, vmem_limit_bytes=56 * 1024 * 1024
        ),
        cost_estimate=pl.CostEstimate(
            flops=6 * total_rows * passage_rows * width,
            bytes_accessed=4 * slots * width,
            transcendentals=2 * total_rows * passage_rows,
        ),
    )(queries[0], passages[0], pattern, positive, owners.transpose(0, 2, 1))
    owned, width_in = encoder_cache.shape[1:]
    hidden_grad, weight_grad, losses, dq = pl.pallas_call(
        owner_kernel,
        out_shape=(
            jax.ShapeDtypeStruct((slots, width_in), bf16),
            jax.ShapeDtypeStruct((width_in, width), f32),
            jax.ShapeDtypeStruct((1, rows), f32),
            jax.ShapeDtypeStruct((rows, width), bf16),
        ),
        in_specs=[hbm] * 5,
        out_specs=(hbm,) * 4,
        scratch_shapes=[
            pltpu.VMEM((slots, width), bf16),
            pltpu.VMEM((owned, width_in), bf16),
            pltpu.VMEM((width_in, width), bf16),
            pltpu.VMEM((slots, width_in), bf16),
            pltpu.VMEM((width_in, width), f32),
            dma((5,)),
            dma((width_in // LANES + 2,)),
        ],
        compiler_params=pltpu.CompilerParams(vmem_limit_bytes=32 * 1024 * 1024),
        cost_estimate=pl.CostEstimate(
            flops=4 * slots * width * width_in,
            bytes_accessed=4 * width * width_in + 8 * slots * width,
            transcendentals=0,
        ),
    )(received, encoder_cache[0], proj_weight, losses, dq)
    return (losses, dq[None], hidden_grad[None], weight_grad[None])


def solution(mesh):
    placed = (
        P("enc", "dp", None),
        P("enc", "dp", None),
        P("enc", "dp", None),
        P("enc", "dp"),
        P("enc", "dp", None),
        P("enc", "dp", None),
        P(),
    )
    return jax.shard_map(
        functools.partial(body, mesh.shape["dp"], mesh.shape["enc"]),
        mesh=mesh,
        in_specs=placed,
        out_specs=(
            P("enc", "dp"),
            P("enc", "dp", None),
            P("enc", "dp", None),
            P("enc", "dp", None),
        ),
        check_vma=False,
    )
```

```python
import functools

import jax
import jax.numpy as jnp
from jax import lax
from jax.experimental import pallas as pl
from jax.experimental.pallas import tpu as pltpu
from jax.sharding import PartitionSpec as P

BLOCK = 128
CH = 32
CAP = 2
CHUNKS = 4
LANES = 256
NEVER = -1e30
INVERSE_COOLNESS = 20.0


def remote(src, dst, send_sem, recv_sem, target):
    return pltpu.make_async_remote_copy(
        src_ref=src,
        dst_ref=dst,
        send_sem=send_sem,
        recv_sem=recv_sem,
        device_id=target,
        device_id_type=pl.DeviceIdType.MESH,
    )


def rows_at(index, count):
    return pl.ds(pl.multiple_of(index * count, count), count)


def group_kernel(
    n_dp, n_enc, q_ref, p_ref, pattern_ref, positive_ref, owners_ref,
    losses_ref, dq_ref, received_ref,
    q_all, p_own, code_out, code_all, e_all, adj, stat_all, dp_sum, outgoing,
    dqs_out, dqs_in, dq_own, dqx_out, dqx_in, select, top_all,
    load_sem, qs_sem, qx_send, qx_recv, qf_send, qf_recv, code_send, code_recv,
    stat_send, stat_recv, dqs_send, dqs_recv, dqx_send, dqx_recv, a2a_send, a2a_recv,
):
    me = lax.axis_index("dp")
    my_owner = lax.axis_index("enc")
    n_pair = n_dp // 2
    pair, core = me // 2, me % 2
    sibling = pair * 2 + 1 - core
    rows, width = q_ref.shape
    passage_rows = p_ref.shape[0]
    blocks = passage_rows // BLOCK
    query_blocks = rows // BLOCK
    span_count = passage_rows // CH
    part = rows // CHUNKS
    slot_rows = CAP * CH

    def dp_target(index):
        return {"dp": index}

    barrier = pltpu.get_barrier_semaphore()
    for k in range(1, n_dp):
        pl.semaphore_signal(
            barrier, inc=1, device_id=dp_target((me + k) % n_dp),
            device_id_type=pl.DeviceIdType.MESH,
        )
    for k in range(1, n_enc):
        pl.semaphore_signal(
            barrier, inc=1, device_id={"enc": (my_owner + k) % n_enc},
            device_id_type=pl.DeviceIdType.MESH,
        )
    load_q = pltpu.make_async_copy(q_ref, q_all.at[rows_at(me, rows)], load_sem.at[0])
    load_p = pltpu.make_async_copy(p_ref, p_own, load_sem.at[1])
    load_q.start()
    load_p.start()
    pl.semaphore_wait(barrier, n_dp + n_enc - 2)

    def chunk(source, h):
        return pl.ds(pl.multiple_of(source * rows + h * part, part), part)

    def query_send(t, h):
        target = ((pair + t) % n_pair) * 2 + core
        return remote(
            q_ref.at[pl.ds(h * part, part)], q_all.at[chunk(me, h)],
            qx_send.at[t, h], qx_recv.at[t, h], dp_target(target),
        )

    def query_arrival(t, h):
        source = ((pair - t + n_pair) % n_pair) * 2 + core
        view = q_all.at[chunk(source, h)]
        return remote(view, view, qx_send.at[t, h], qx_recv.at[t, h], dp_target(source))

    def query_forward(t, h, owner_core):
        source = ((pair - t + n_pair) % n_pair) * 2 + owner_core
        view = q_all.at[chunk(source, h)]
        return remote(view, view, qf_send.at[t, h], qf_recv.at[t, h], dp_target(sibling))

    for h in range(CHUNKS):
        for t in range(1, n_pair):
            query_send(t, h).start()
    to_sibling = remote(
        q_ref, q_all.at[rows_at(me, rows)], qs_sem.at[0], qs_sem.at[1], dp_target(sibling)
    )
    to_sibling.start()

    code_out[...] = jnp.zeros_like(code_out)
    for b in range(query_blocks):
        for j in range(n_dp * blocks):
            hit = (positive_ref[0, b] == j).astype(jnp.int32)
            seen = (pattern_ref[0, b, j] == 1).astype(jnp.int32)
            value = jnp.maximum(2 * hit, seen).astype(jnp.float32)
            code_out[j // blocks, j % blocks : j % blocks + 1, b * BLOCK : (b + 1) * BLOCK] = (
                jnp.full((1, BLOCK), value, jnp.float32)
            )
    code_all[me] = code_out[me]

    def code_copy(k):
        target = (me + k) % n_dp
        return remote(
            code_out.at[target], code_all.at[me], code_send.at[k], code_recv.at[k],
            dp_target(target),
        )

    for k in range(1, n_dp):
        code_copy(k).start()

    def select_spans(owner, carry):
        seen = jnp.int32(0)
        found = [jnp.int32(-1)] * CAP
        for c in range(span_count):
            hit = (owners_ref[0, 0, c] == owner).astype(jnp.int32)
            for r in range(CAP):
                found[r] = found[r] + (c + 1) * hit * (seen == r).astype(jnp.int32)
            seen = seen + hit
        line = lax.broadcasted_iota(jnp.int32, (CH, passage_rows), 0)
        column = lax.broadcasted_iota(jnp.int32, (CH, passage_rows), 1)
        for r in range(CAP):
            chosen = (column == line + found[r] * CH).astype(jnp.float32)
            select[rows_at(owner * CAP + r, CH), :] = chosen.astype(jnp.bfloat16)
        return carry

    lax.fori_loop(0, n_enc, select_spans, 0)

    on_diagonal = (
        lax.broadcasted_iota(jnp.int32, (BLOCK, rows), 0)
        == lax.broadcasted_iota(jnp.int32, (BLOCK, rows), 1) % BLOCK
    )

    def score(source):
        columns = rows_at(source, rows)
        scores = lax.dot_general(
            p_own[...], q_all[columns, :], (((1,), (1,)), ((), ())),
            preferred_element_type=jnp.float32,
        ) * INVERSE_COOLNESS
        top = jnp.full((1, rows), NEVER, jnp.float32)
        picked = jnp.zeros((1, rows), jnp.float32)
        masked = []
        for j in range(blocks):
            block = scores[j * BLOCK : (j + 1) * BLOCK, :]
            code = code_all[source, j : j + 1, :]
            block_masked = jnp.where(code > 0.5, block, NEVER)
            masked.append(block_masked)
            top = jnp.maximum(top, jnp.max(block_masked, axis=0, keepdims=True))
            hit = on_diagonal & (code > 1.5)
            picked = picked + jnp.sum(jnp.where(hit, block, 0.0), axis=0, keepdims=True)
        shift = jnp.where(top > 0.5 * NEVER, top, 0.0)
        total = jnp.zeros((1, rows), jnp.float32)
        for j in range(blocks):
            terms = jnp.exp(masked[j] - shift)
            e_all[j * BLOCK : (j + 1) * BLOCK, columns] = terms
            total = total + jnp.sum(terms, axis=0, keepdims=True)
        top_all[0:1, columns] = top
        stat_all[me, 0:1, columns] = jnp.where(
            total > 0.0, shift + jnp.log(jnp.maximum(total, 1e-30)), NEVER
        )
        stat_all[me, 1:2, columns] = picked

    load_q.wait()
    load_p.wait()

    def code_wait(k):
        source = (me - k + n_dp) % n_dp
        remote(
            code_out.at[0], code_all.at[source], code_send.at[k], code_recv.at[k],
            dp_target(source),
        ).wait_recv()

    score(me)
    remote(
        q_ref, q_all.at[rows_at(sibling, rows)], qs_sem.at[0], qs_sem.at[1], dp_target(sibling)
    ).wait_recv()
    for k in range(1, n_dp):
        code_wait(k)
    score(sibling)

    def take(t, carry):
        first = ((pair - t + n_pair) % n_pair) * 2
        for h in range(CHUNKS):
            query_arrival(t, h).wait_recv()
            query_forward(t, h, core).start()
        score(first + core)
        for h in range(CHUNKS):
            query_forward(t, h, 1 - core).wait_recv()
        score(first + 1 - core)
        return carry

    lax.fori_loop(1, n_pair, take, 0)

    def stat_copy(k, source, target):
        view = stat_all.at[source]
        return remote(view, view, stat_send.at[k], stat_recv.at[k], dp_target(target))

    for k in range(1, n_dp):
        stat_copy(k, me, (me + k) % n_dp).start()
    for k in range(1, n_dp):
        stat_copy(k, (me - k + n_dp) % n_dp, me).wait_recv()

    def adjust(source, carry):
        columns = rows_at(source, rows)
        parts = [stat_all[d, 0:1, columns] for d in range(n_dp)]
        top = functools.reduce(jnp.maximum, parts)
        total = functools.reduce(jnp.add, [jnp.exp(x - top) for x in parts])
        log_total = top + jnp.log(total)
        factor = jnp.exp(top_all[0:1, columns] - log_total)
        for j in range(blocks):
            lines = slice(j * BLOCK, (j + 1) * BLOCK)
            hit = on_diagonal & (code_all[source, j : j + 1, :] > 1.5)
            probability = e_all[lines, columns] * factor
            adj[lines, columns] = (probability - jnp.where(hit, 1.0, 0.0)).astype(jnp.bfloat16)
        return carry

    lax.fori_loop(0, n_dp, adjust, 0)

    def span_copy(k, owner, place):
        return remote(
            outgoing.at[rows_at(owner, slot_rows)], received_ref.at[rows_at(place, slot_rows)],
            a2a_send.at[k], a2a_recv.at[k], {"enc": owner},
        )

    depth = min(n_dp * rows, 1024)
    for n in range(width // LANES):
        lanes = slice(n * LANES, (n + 1) * LANES)
        if depth == n_dp * rows:
            total = jnp.dot(adj[...], q_all[:, lanes], preferred_element_type=jnp.float32)
        else:
            dp_sum[...] = jnp.zeros_like(dp_sum)

            def add_group(g, carry, lanes=lanes):
                inner = rows_at(g, depth)
                dp_sum[...] += jnp.dot(
                    adj[:, inner], q_all[inner, lanes], preferred_element_type=jnp.float32
                )
                return carry

            lax.fori_loop(0, n_dp * rows // depth, add_group, 0)
            total = dp_sum[...]
        grad = (total * INVERSE_COOLNESS).astype(jnp.bfloat16)
        outgoing[:, lanes] = jnp.dot(
            select[...], grad, preferred_element_type=jnp.float32
        ).astype(jnp.bfloat16)

    def send_spans(k, carry):
        span_copy(k, (my_owner + k) % n_enc, my_owner).start()
        return carry

    lax.fori_loop(1, n_enc, send_spans, 0)
    keep = pltpu.make_async_copy(
        outgoing.at[rows_at(my_owner, slot_rows)],
        received_ref.at[rows_at(my_owner, slot_rows)],
        load_sem.at[2],
    )
    keep.start()

    def partial(source):
        return lax.dot_general(
            adj[:, rows_at(source, rows)], p_own[...], (((0,), (0,)), ((), ())),
            preferred_element_type=jnp.float32,
        )

    def dqs_copy(t):
        return remote(
            dqs_out.at[t], dqs_in.at[t], dqs_send.at[t], dqs_recv.at[t], dp_target(sibling)
        )

    def dqx_copy(t):
        target = ((pair + t) % n_pair) * 2 + core
        return remote(
            dqx_out.at[t], dqx_in.at[t], dqx_send.at[t], dqx_recv.at[t], dp_target(target)
        )

    def sibling_share(t, carry):
        target = ((pair + t) % n_pair) * 2
        dqs_out[t] = partial(target + 1 - core).astype(jnp.bfloat16)
        dqs_copy(t).start()
        return carry

    def chip_share(t, carry):
        target = ((pair + t) % n_pair) * 2
        dq_own[...] = partial(target + core)
        dqs_copy(t).wait_recv()
        dqx_out[t] = (dq_own[...] + dqs_in[t].astype(jnp.float32)).astype(jnp.bfloat16)
        dqx_copy(t).start()
        return carry

    lax.fori_loop(1, n_pair, sibling_share, 0)
    lax.fori_loop(1, n_pair, chip_share, 0)
    sibling_share(0, 0)
    dq_own[...] = partial(me)
    dqs_copy(0).wait_recv()
    dq_own[...] += dqs_in[0].astype(jnp.float32)

    own = rows_at(me, rows)
    parts = [stat_all[d, 0:1, own] for d in range(n_dp)]
    top = functools.reduce(jnp.maximum, parts)
    total = functools.reduce(jnp.add, [jnp.exp(x - top) for x in parts])
    picked = functools.reduce(jnp.add, [stat_all[d, 1:2, own] for d in range(n_dp)])
    losses_ref[...] = top + jnp.log(total) - picked

    def add_chip(t, carry):
        dqx_copy(t).wait_recv()
        dq_own[...] += dqx_in[t].astype(jnp.float32)
        return carry

    lax.fori_loop(1, n_pair, add_chip, 0)
    dq_ref[...] = (dq_own[...] * INVERSE_COOLNESS).astype(jnp.bfloat16)

    to_sibling.wait_send()
    for t in range(1, n_pair):
        for h in range(CHUNKS):
            query_send(t, h).wait_send()
            query_forward(t, h, core).wait_send()
    for k in range(1, n_dp):
        code_copy(k).wait_send()
        stat_copy(k, me, (me + k) % n_dp).wait_send()
    for t in range(n_pair):
        dqs_copy(t).wait_send()
        if t:
            dqx_copy(t).wait_send()
    for k in range(1, n_enc):
        span_copy(k, (my_owner + k) % n_enc, my_owner).wait_send()
        source = (my_owner - k + n_enc) % n_enc
        span_copy(k, source, source).wait_recv()
    keep.wait()


def owner_kernel(
    received_ref, cache_ref, weight_ref, losses_in, dq_in,
    hidden_ref, grad_ref, losses_ref, dq_ref,
    received, cache, weight, hidden, grad, in_sem, out_sem,
):
    loads = [
        pltpu.make_async_copy(source, place, in_sem.at[i])
        for i, (source, place) in enumerate(
            [
                (received_ref, received),
                (cache_ref, cache),
                (weight_ref, weight),
                (dq_in, dq_ref),
                (losses_in, losses_ref),
            ]
        )
    ]
    for load in loads:
        load.start()
    loads[0].wait()
    loads[1].wait()
    stores = []

    def store(source, place, lines):
        copy = pltpu.make_async_copy(
            source.at[lines], place.at[lines], out_sem.at[len(stores)]
        )
        copy.start()
        stores.append(copy)

    for n in range(0, cache.shape[1], LANES):
        lines = pl.ds(n, LANES)
        grad[lines, :] = lax.dot_general(
            cache[:, lines], received[...], (((0,), (0,)), ((), ())),
            preferred_element_type=jnp.float32,
        )
        store(grad, grad_ref, lines)
    loads[2].wait()
    part = received.shape[0] // 2
    for n in range(2):
        lines = pl.ds(n * part, part)
        hidden[lines, :] = lax.dot_general(
            received[lines, :], weight[...], (((1,), (1,)), ((), ())),
            preferred_element_type=jnp.float32,
        ).astype(jnp.bfloat16)
        store(hidden, hidden_ref, lines)
    loads[3].wait()
    loads[4].wait()
    for copy in stores:
        copy.wait()


def body(n_dp, n_enc, queries, passages, pattern, positive, owners, encoder_cache, proj_weight):
    rows, width = queries.shape[1:]
    passage_rows = passages.shape[1]
    blocks = passage_rows // BLOCK
    code_rows = -(-blocks // 4) * 4
    n_pair = n_dp // 2
    total_rows = n_dp * rows
    slots = n_enc * CAP * CH
    bf16, f32 = jnp.bfloat16, jnp.float32
    dma = pltpu.SemaphoreType.DMA
    smem = pl.BlockSpec(memory_space=pltpu.SMEM)
    vmem = pl.BlockSpec(memory_space=pltpu.VMEM)
    hbm = pl.BlockSpec(memory_space=pl.ANY)
    losses, dq, received = pl.pallas_call(
        functools.partial(group_kernel, n_dp, n_enc),
        out_shape=(
            jax.ShapeDtypeStruct((1, rows), f32),
            jax.ShapeDtypeStruct((rows, width), bf16),
            jax.ShapeDtypeStruct((slots, width), bf16),
        ),
        in_specs=[hbm, hbm, smem, smem, smem],
        out_specs=(vmem, vmem, hbm),
        scratch_shapes=[
            pltpu.VMEM((total_rows, width), bf16),
            pltpu.VMEM((passage_rows, width), bf16),
            pltpu.VMEM((n_dp, code_rows, rows), f32),
            pltpu.VMEM((n_dp, code_rows, rows), f32),
            pltpu.VMEM((passage_rows, total_rows), f32),
            pltpu.VMEM((passage_rows, total_rows), bf16),
            pltpu.VMEM((n_dp, 2, total_rows), f32),
            pltpu.VMEM((passage_rows, LANES), f32),
            pltpu.VMEM((slots, width), bf16),
            pltpu.VMEM((n_pair, rows, width), bf16),
            pltpu.VMEM((n_pair, rows, width), bf16),
            pltpu.VMEM((rows, width), f32),
            pltpu.VMEM((n_pair, rows, width), bf16),
            pltpu.VMEM((n_pair, rows, width), bf16),
            pltpu.VMEM((slots, passage_rows), bf16),
            pltpu.VMEM((1, total_rows), f32),
            dma((3,)),
            dma((2,)),
            dma((n_pair, CHUNKS)),
            dma((n_pair, CHUNKS)),
            dma((n_pair, CHUNKS)),
            dma((n_pair, CHUNKS)),
            dma((n_dp,)),
            dma((n_dp,)),
            dma((n_dp,)),
            dma((n_dp,)),
            dma((n_pair,)),
            dma((n_pair,)),
            dma((n_pair,)),
            dma((n_pair,)),
            dma((n_enc,)),
            dma((n_enc,)),
        ],
        compiler_params=pltpu.CompilerParams(
            collective_id=0, has_side_effects=True, vmem_limit_bytes=56 * 1024 * 1024
        ),
        cost_estimate=pl.CostEstimate(
            flops=6 * total_rows * passage_rows * width,
            bytes_accessed=4 * slots * width,
            transcendentals=2 * total_rows * passage_rows,
        ),
    )(queries[0], passages[0], pattern, positive, owners.transpose(0, 2, 1))
    owned, width_in = encoder_cache.shape[1:]
    hidden_grad, weight_grad, losses, dq = pl.pallas_call(
        owner_kernel,
        out_shape=(
            jax.ShapeDtypeStruct((slots, width_in), bf16),
            jax.ShapeDtypeStruct((width_in, width), f32),
            jax.ShapeDtypeStruct((1, rows), f32),
            jax.ShapeDtypeStruct((rows, width), bf16),
        ),
        in_specs=[hbm] * 5,
        out_specs=(hbm,) * 4,
        scratch_shapes=[
            pltpu.VMEM((slots, width), bf16),
            pltpu.VMEM((owned, width_in), bf16),
            pltpu.VMEM((width_in, width), bf16),
            pltpu.VMEM((slots, width_in), bf16),
            pltpu.VMEM((width_in, width), f32),
            dma((5,)),
            dma((width_in // LANES + 2,)),
        ],
        compiler_params=pltpu.CompilerParams(vmem_limit_bytes=56 * 1024 * 1024),
        cost_estimate=pl.CostEstimate(
            flops=4 * slots * width * width_in,
            bytes_accessed=4 * width * width_in + 8 * slots * width,
            transcendentals=0,
        ),
    )(received, encoder_cache[0], proj_weight, losses, dq)
    return (losses, dq[None], hidden_grad[None], weight_grad[None])


def solution(mesh):
    placed = (
        P("enc", "dp", None),
        P("enc", "dp", None),
        P("enc", "dp", None),
        P("enc", "dp"),
        P("enc", "dp", None),
        P("enc", "dp", None),
        P(),
    )
    return jax.shard_map(
        functools.partial(body, mesh.shape["dp"], mesh.shape["enc"]),
        mesh=mesh,
        in_specs=placed,
        out_specs=(
            P("enc", "dp"),
            P("enc", "dp", None),
            P("enc", "dp", None),
            P("enc", "dp", None),
        ),
        check_vma=False,
    )
```

```python
import functools

import jax
import jax.numpy as jnp
from jax import lax
from jax.experimental import pallas as pl
from jax.experimental.pallas import tpu as pltpu
from jax.sharding import PartitionSpec as P

BLOCK = 128
CH = 32
CAP = 2
CHUNKS = 4
LANES = 256
NEVER = -1e30
INVERSE_COOLNESS = 20.0


def remote(src, dst, send_sem, recv_sem, target):
    return pltpu.make_async_remote_copy(
        src_ref=src,
        dst_ref=dst,
        send_sem=send_sem,
        recv_sem=recv_sem,
        device_id=target,
        device_id_type=pl.DeviceIdType.MESH,
    )


def rows_at(index, count):
    return pl.ds(pl.multiple_of(index * count, count), count)


def group_kernel(
    n_dp, n_enc, q_ref, p_ref, pattern_ref, positive_ref, owners_ref,
    losses_ref, dq_ref, received_ref,
    q_all, p_own, code_out, code_all, e_all, adj, stat_all, dp_sum, outgoing,
    dqs_out, dqs_in, dq_own, dqx_out, dqx_in, select, top_all,
    load_sem, qs_sem, qx_send, qx_recv, qf_send, qf_recv, code_send, code_recv,
    stat_send, stat_recv, dqs_send, dqs_recv, dqx_send, dqx_recv, a2a_send, a2a_recv,
):
    me = lax.axis_index("dp")
    my_owner = lax.axis_index("enc")
    n_pair = n_dp // 2
    pair, core = me // 2, me % 2
    sibling = pair * 2 + 1 - core
    rows, width = q_ref.shape
    passage_rows = p_ref.shape[0]
    blocks = passage_rows // BLOCK
    query_blocks = rows // BLOCK
    span_count = passage_rows // CH
    part = rows // CHUNKS
    slot_rows = CAP * CH

    def dp_target(index):
        return {"dp": index}

    barrier = pltpu.get_barrier_semaphore()
    for k in range(1, n_dp):
        pl.semaphore_signal(
            barrier, inc=1, device_id=dp_target((me + k) % n_dp),
            device_id_type=pl.DeviceIdType.MESH,
        )
    for k in range(1, n_enc):
        pl.semaphore_signal(
            barrier, inc=1, device_id={"enc": (my_owner + k) % n_enc},
            device_id_type=pl.DeviceIdType.MESH,
        )
    load_q = pltpu.make_async_copy(q_ref, q_all.at[rows_at(me, rows)], load_sem.at[0])
    load_p = pltpu.make_async_copy(p_ref, p_own, load_sem.at[1])
    load_q.start()
    load_p.start()
    pl.semaphore_wait(barrier, n_dp + n_enc - 2)

    def chunk(source, h):
        return pl.ds(pl.multiple_of(source * rows + h * part, part), part)

    def query_send(t, h):
        target = ((pair + t) % n_pair) * 2 + core
        return remote(
            q_ref.at[pl.ds(h * part, part)], q_all.at[chunk(me, h)],
            qx_send.at[t, h], qx_recv.at[t, h], dp_target(target),
        )

    def query_arrival(t, h):
        source = ((pair - t + n_pair) % n_pair) * 2 + core
        view = q_all.at[chunk(source, h)]
        return remote(view, view, qx_send.at[t, h], qx_recv.at[t, h], dp_target(source))

    def query_forward(t, h, owner_core):
        source = ((pair - t + n_pair) % n_pair) * 2 + owner_core
        view = q_all.at[chunk(source, h)]
        return remote(view, view, qf_send.at[t, h], qf_recv.at[t, h], dp_target(sibling))

    for h in range(CHUNKS):
        for t in range(1, n_pair):
            query_send(t, h).start()
    to_sibling = remote(
        q_ref, q_all.at[rows_at(me, rows)], qs_sem.at[0], qs_sem.at[1], dp_target(sibling)
    )
    to_sibling.start()

    code_out[...] = jnp.zeros_like(code_out)
    for b in range(query_blocks):
        for j in range(n_dp * blocks):
            hit = (positive_ref[0, b] == j).astype(jnp.int32)
            seen = (pattern_ref[0, b, j] == 1).astype(jnp.int32)
            value = jnp.maximum(2 * hit, seen).astype(jnp.float32)
            code_out[j // blocks, j % blocks : j % blocks + 1, b * BLOCK : (b + 1) * BLOCK] = (
                jnp.full((1, BLOCK), value, jnp.float32)
            )
    code_all[me] = code_out[me]

    def code_copy(k):
        target = (me + k) % n_dp
        return remote(
            code_out.at[target], code_all.at[me], code_send.at[k], code_recv.at[k],
            dp_target(target),
        )

    for k in range(1, n_dp):
        code_copy(k).start()

    def select_spans(owner, carry):
        seen = jnp.int32(0)
        found = [jnp.int32(-1)] * CAP
        for c in range(span_count):
            hit = (owners_ref[0, 0, c] == owner).astype(jnp.int32)
            for r in range(CAP):
                found[r] = found[r] + (c + 1) * hit * (seen == r).astype(jnp.int32)
            seen = seen + hit
        line = lax.broadcasted_iota(jnp.int32, (CH, passage_rows), 0)
        column = lax.broadcasted_iota(jnp.int32, (CH, passage_rows), 1)
        for r in range(CAP):
            chosen = (column == line + found[r] * CH).astype(jnp.float32)
            select[rows_at(owner * CAP + r, CH), :] = chosen.astype(jnp.bfloat16)
        return carry

    lax.fori_loop(0, n_enc, select_spans, 0)

    on_diagonal = (
        lax.broadcasted_iota(jnp.int32, (BLOCK, rows), 0)
        == lax.broadcasted_iota(jnp.int32, (BLOCK, rows), 1) % BLOCK
    )

    def score(source):
        columns = rows_at(source, rows)
        scores = lax.dot_general(
            p_own[...], q_all[columns, :], (((1,), (1,)), ((), ())),
            preferred_element_type=jnp.float32,
        ) * INVERSE_COOLNESS
        top = jnp.full((1, rows), NEVER, jnp.float32)
        picked = jnp.zeros((1, rows), jnp.float32)
        masked = []
        for j in range(blocks):
            block = scores[j * BLOCK : (j + 1) * BLOCK, :]
            code = code_all[source, j : j + 1, :]
            block_masked = jnp.where(code > 0.5, block, NEVER)
            masked.append(block_masked)
            top = jnp.maximum(top, jnp.max(block_masked, axis=0, keepdims=True))
            hit = on_diagonal & (code > 1.5)
            picked = picked + jnp.sum(jnp.where(hit, block, 0.0), axis=0, keepdims=True)
        shift = jnp.where(top > 0.5 * NEVER, top, 0.0)
        total = jnp.zeros((1, rows), jnp.float32)
        for j in range(blocks):
            terms = jnp.exp(masked[j] - shift)
            e_all[j * BLOCK : (j + 1) * BLOCK, columns] = terms
            total = total + jnp.sum(terms, axis=0, keepdims=True)
        top_all[0:1, columns] = top
        stat_all[me, 0:1, columns] = jnp.where(
            total > 0.0, shift + jnp.log(jnp.maximum(total, 1e-30)), NEVER
        )
        stat_all[me, 1:2, columns] = picked

    load_q.wait()
    load_p.wait()

    def code_wait(k):
        source = (me - k + n_dp) % n_dp
        remote(
            code_out.at[0], code_all.at[source], code_send.at[k], code_recv.at[k],
            dp_target(source),
        ).wait_recv()

    score(me)
    remote(
        q_ref, q_all.at[rows_at(sibling, rows)], qs_sem.at[0], qs_sem.at[1], dp_target(sibling)
    ).wait_recv()
    for k in range(1, n_dp):
        code_wait(k)
    score(sibling)

    def take(t, carry):
        first = ((pair - t + n_pair) % n_pair) * 2
        for h in range(CHUNKS):
            query_arrival(t, h).wait_recv()
            query_forward(t, h, core).start()
        score(first + core)
        for h in range(CHUNKS):
            query_forward(t, h, 1 - core).wait_recv()
        score(first + 1 - core)
        return carry

    lax.fori_loop(1, n_pair, take, 0)

    def stat_copy(k, source, target):
        view = stat_all.at[source]
        return remote(view, view, stat_send.at[k], stat_recv.at[k], dp_target(target))

    for k in range(1, n_dp):
        stat_copy(k, me, (me + k) % n_dp).start()
    for k in range(1, n_dp):
        stat_copy(k, (me - k + n_dp) % n_dp, me).wait_recv()

    def adjust(source, carry):
        columns = rows_at(source, rows)
        parts = [stat_all[d, 0:1, columns] for d in range(n_dp)]
        top = functools.reduce(jnp.maximum, parts)
        total = functools.reduce(jnp.add, [jnp.exp(x - top) for x in parts])
        log_total = top + jnp.log(total)
        factor = jnp.exp(top_all[0:1, columns] - log_total)
        for j in range(blocks):
            lines = slice(j * BLOCK, (j + 1) * BLOCK)
            hit = on_diagonal & (code_all[source, j : j + 1, :] > 1.5)
            probability = e_all[lines, columns] * factor
            adj[lines, columns] = (probability - jnp.where(hit, 1.0, 0.0)).astype(jnp.bfloat16)
        return carry

    lax.fori_loop(0, n_dp, adjust, 0)

    half = n_enc // 2
    my_half, my_place = my_owner // half, my_owner % half
    turns = [(0, True)]
    for j in range(1, half):
        turns += [(j, False), (j, True)]

    def owner_at(j, across):
        side = (1 - my_half) if across else my_half
        return side * half + (my_place + j + half) % half

    def span_copy(j, across, owner, place):
        sem = j if across else j + half
        return remote(
            outgoing.at[rows_at(owner, slot_rows)], received_ref.at[rows_at(place, slot_rows)],
            a2a_send.at[sem], a2a_recv.at[sem], {"enc": owner},
        )

    depth = min(n_dp * rows, 1024)
    for n in range(width // LANES):
        lanes = slice(n * LANES, (n + 1) * LANES)
        if depth == n_dp * rows:
            total = jnp.dot(adj[...], q_all[:, lanes], preferred_element_type=jnp.float32)
        else:
            dp_sum[...] = jnp.zeros_like(dp_sum)

            def add_group(g, carry, lanes=lanes):
                inner = rows_at(g, depth)
                dp_sum[...] += jnp.dot(
                    adj[:, inner], q_all[inner, lanes], preferred_element_type=jnp.float32
                )
                return carry

            lax.fori_loop(0, n_dp * rows // depth, add_group, 0)
            total = dp_sum[...]
        grad = (total * INVERSE_COOLNESS).astype(jnp.bfloat16)
        outgoing[:, lanes] = jnp.dot(
            select[...], grad, preferred_element_type=jnp.float32
        ).astype(jnp.bfloat16)

    for j, across in turns:
        span_copy(j, across, owner_at(j, across), my_owner).start()
    keep = pltpu.make_async_copy(
        outgoing.at[rows_at(my_owner, slot_rows)],
        received_ref.at[rows_at(my_owner, slot_rows)],
        load_sem.at[2],
    )
    keep.start()

    def partial(source):
        return lax.dot_general(
            adj[:, rows_at(source, rows)], p_own[...], (((0,), (0,)), ((), ())),
            preferred_element_type=jnp.float32,
        )

    def dqs_copy(t):
        return remote(
            dqs_out.at[t], dqs_in.at[t], dqs_send.at[t], dqs_recv.at[t], dp_target(sibling)
        )

    def dqx_copy(t):
        target = ((pair + t) % n_pair) * 2 + core
        return remote(
            dqx_out.at[t], dqx_in.at[t], dqx_send.at[t], dqx_recv.at[t], dp_target(target)
        )

    def sibling_share(t, carry):
        target = ((pair + t) % n_pair) * 2
        dqs_out[t] = partial(target + 1 - core).astype(jnp.bfloat16)
        dqs_copy(t).start()
        return carry

    def chip_share(t, carry):
        target = ((pair + t) % n_pair) * 2
        dq_own[...] = partial(target + core)
        dqs_copy(t).wait_recv()
        dqx_out[t] = (dq_own[...] + dqs_in[t].astype(jnp.float32)).astype(jnp.bfloat16)
        dqx_copy(t).start()
        return carry

    lax.fori_loop(1, n_pair, sibling_share, 0)
    lax.fori_loop(1, n_pair, chip_share, 0)
    sibling_share(0, 0)
    dq_own[...] = partial(me)
    dqs_copy(0).wait_recv()
    dq_own[...] += dqs_in[0].astype(jnp.float32)

    own = rows_at(me, rows)
    parts = [stat_all[d, 0:1, own] for d in range(n_dp)]
    top = functools.reduce(jnp.maximum, parts)
    total = functools.reduce(jnp.add, [jnp.exp(x - top) for x in parts])
    picked = functools.reduce(jnp.add, [stat_all[d, 1:2, own] for d in range(n_dp)])
    losses_ref[...] = top + jnp.log(total) - picked

    def add_chip(t, carry):
        dqx_copy(t).wait_recv()
        dq_own[...] += dqx_in[t].astype(jnp.float32)
        return carry

    lax.fori_loop(1, n_pair, add_chip, 0)
    dq_ref[...] = (dq_own[...] * INVERSE_COOLNESS).astype(jnp.bfloat16)

    to_sibling.wait_send()
    for t in range(1, n_pair):
        for h in range(CHUNKS):
            query_send(t, h).wait_send()
            query_forward(t, h, core).wait_send()
    for k in range(1, n_dp):
        code_copy(k).wait_send()
        stat_copy(k, me, (me + k) % n_dp).wait_send()
    for t in range(n_pair):
        dqs_copy(t).wait_send()
        if t:
            dqx_copy(t).wait_send()
    for j, across in turns:
        span_copy(j, across, owner_at(j, across), my_owner).wait_send()
        source = owner_at(-j, across)
        span_copy(j, across, source, source).wait_recv()
    keep.wait()


def owner_kernel(
    received_ref, cache_ref, weight_ref, losses_in, dq_in,
    hidden_ref, grad_ref, losses_ref, dq_ref,
    received, cache, weight, hidden, grad, dq, losses, in_sem, out_sem,
):
    loads = [
        pltpu.make_async_copy(source, place, in_sem.at[i])
        for i, (source, place) in enumerate(
            [
                (received_ref, received),
                (cache_ref, cache),
                (weight_ref, weight),
                (dq_in, dq),
                (losses_in, losses),
            ]
        )
    ]
    for load in loads:
        load.start()
    loads[0].wait()
    loads[1].wait()
    stores = []

    def store(source, place, lines):
        copy = pltpu.make_async_copy(
            source.at[lines], place.at[lines], out_sem.at[len(stores)]
        )
        copy.start()
        stores.append(copy)

    for n in range(0, cache.shape[1], LANES):
        lines = pl.ds(n, LANES)
        grad[lines, :] = lax.dot_general(
            cache[:, lines], received[...], (((0,), (0,)), ((), ())),
            preferred_element_type=jnp.float32,
        )
        store(grad, grad_ref, lines)
    loads[3].wait()
    store(dq, dq_ref, pl.ds(0, dq.shape[0]))
    loads[4].wait()
    store(losses, losses_ref, pl.ds(0, 1))
    loads[2].wait()
    part = received.shape[0] // 2
    for n in range(2):
        lines = pl.ds(n * part, part)
        hidden[lines, :] = lax.dot_general(
            received[lines, :], weight[...], (((1,), (1,)), ((), ())),
            preferred_element_type=jnp.float32,
        ).astype(jnp.bfloat16)
        store(hidden, hidden_ref, lines)
    for copy in stores:
        copy.wait()


def body(n_dp, n_enc, queries, passages, pattern, positive, owners, encoder_cache, proj_weight):
    rows, width = queries.shape[1:]
    passage_rows = passages.shape[1]
    blocks = passage_rows // BLOCK
    code_rows = -(-blocks // 4) * 4
    n_pair = n_dp // 2
    total_rows = n_dp * rows
    slots = n_enc * CAP * CH
    bf16, f32 = jnp.bfloat16, jnp.float32
    dma = pltpu.SemaphoreType.DMA
    smem = pl.BlockSpec(memory_space=pltpu.SMEM)
    vmem = pl.BlockSpec(memory_space=pltpu.VMEM)
    hbm = pl.BlockSpec(memory_space=pl.ANY)
    losses, dq, received = pl.pallas_call(
        functools.partial(group_kernel, n_dp, n_enc),
        out_shape=(
            jax.ShapeDtypeStruct((1, rows), f32),
            jax.ShapeDtypeStruct((rows, width), bf16),
            jax.ShapeDtypeStruct((slots, width), bf16),
        ),
        in_specs=[hbm, hbm, smem, smem, smem],
        out_specs=(vmem, vmem, hbm),
        scratch_shapes=[
            pltpu.VMEM((total_rows, width), bf16),
            pltpu.VMEM((passage_rows, width), bf16),
            pltpu.VMEM((n_dp, code_rows, rows), f32),
            pltpu.VMEM((n_dp, code_rows, rows), f32),
            pltpu.VMEM((passage_rows, total_rows), f32),
            pltpu.VMEM((passage_rows, total_rows), bf16),
            pltpu.VMEM((n_dp, 2, total_rows), f32),
            pltpu.VMEM((passage_rows, LANES), f32),
            pltpu.VMEM((slots, width), bf16),
            pltpu.VMEM((n_pair, rows, width), bf16),
            pltpu.VMEM((n_pair, rows, width), bf16),
            pltpu.VMEM((rows, width), f32),
            pltpu.VMEM((n_pair, rows, width), bf16),
            pltpu.VMEM((n_pair, rows, width), bf16),
            pltpu.VMEM((slots, passage_rows), bf16),
            pltpu.VMEM((1, total_rows), f32),
            dma((3,)),
            dma((2,)),
            dma((n_pair, CHUNKS)),
            dma((n_pair, CHUNKS)),
            dma((n_pair, CHUNKS)),
            dma((n_pair, CHUNKS)),
            dma((n_dp,)),
            dma((n_dp,)),
            dma((n_dp,)),
            dma((n_dp,)),
            dma((n_pair,)),
            dma((n_pair,)),
            dma((n_pair,)),
            dma((n_pair,)),
            dma((n_enc,)),
            dma((n_enc,)),
        ],
        compiler_params=pltpu.CompilerParams(
            collective_id=0, has_side_effects=True, vmem_limit_bytes=56 * 1024 * 1024
        ),
        cost_estimate=pl.CostEstimate(
            flops=6 * total_rows * passage_rows * width,
            bytes_accessed=4 * slots * width,
            transcendentals=2 * total_rows * passage_rows,
        ),
    )(queries[0], passages[0], pattern, positive, owners.transpose(0, 2, 1))
    owned, width_in = encoder_cache.shape[1:]
    hidden_grad, weight_grad, losses, dq = pl.pallas_call(
        owner_kernel,
        out_shape=(
            jax.ShapeDtypeStruct((slots, width_in), bf16),
            jax.ShapeDtypeStruct((width_in, width), f32),
            jax.ShapeDtypeStruct((1, rows), f32),
            jax.ShapeDtypeStruct((rows, width), bf16),
        ),
        in_specs=[hbm] * 5,
        out_specs=(hbm,) * 4,
        scratch_shapes=[
            pltpu.VMEM((slots, width), bf16),
            pltpu.VMEM((owned, width_in), bf16),
            pltpu.VMEM((width_in, width), bf16),
            pltpu.VMEM((slots, width_in), bf16),
            pltpu.VMEM((width_in, width), f32),
            pltpu.VMEM((rows, width), bf16),
            pltpu.VMEM((1, rows), f32),
            dma((5,)),
            dma((width_in // LANES + 4,)),
        ],
        compiler_params=pltpu.CompilerParams(vmem_limit_bytes=56 * 1024 * 1024),
        cost_estimate=pl.CostEstimate(
            flops=4 * slots * width * width_in,
            bytes_accessed=4 * width * width_in + 8 * slots * width,
            transcendentals=0,
        ),
    )(received, encoder_cache[0], proj_weight, losses, dq)
    return (losses, dq[None], hidden_grad[None], weight_grad[None])


def solution(mesh):
    placed = (
        P("enc", "dp", None),
        P("enc", "dp", None),
        P("enc", "dp", None),
        P("enc", "dp"),
        P("enc", "dp", None),
        P("enc", "dp", None),
        P(),
    )
    return jax.shard_map(
        functools.partial(body, mesh.shape["dp"], mesh.shape["enc"]),
        mesh=mesh,
        in_specs=placed,
        out_specs=(
            P("enc", "dp"),
            P("enc", "dp", None),
            P("enc", "dp", None),
            P("enc", "dp", None),
        ),
        check_vma=False,
    )
```

```python
import functools

import jax
import jax.numpy as jnp
from jax import lax
from jax.experimental import pallas as pl
from jax.experimental.pallas import tpu as pltpu
from jax.sharding import PartitionSpec as P

BLOCK = 128
CH = 32
CAP = 2
CHUNKS = 4
LANES = 256
NEVER = -1e30
INVERSE_COOLNESS = 20.0


def remote(src, dst, send_sem, recv_sem, target):
    return pltpu.make_async_remote_copy(
        src_ref=src,
        dst_ref=dst,
        send_sem=send_sem,
        recv_sem=recv_sem,
        device_id=target,
        device_id_type=pl.DeviceIdType.MESH,
    )


def rows_at(index, count):
    return pl.ds(pl.multiple_of(index * count, count), count)


def group_kernel(
    n_dp, n_enc, q_ref, p_ref, pattern_ref, positive_ref, owners_ref,
    losses_ref, dq_ref, received_ref,
    q_all, p_own, code_out, code_all, e_all, adj, stat_all, dp_sum, outgoing,
    dqs_out, dqs_in, dq_own, dqx_out, dqx_in, select, top_all,
    load_sem, qs_sem, qx_send, qx_recv, qf_send, qf_recv, code_send, code_recv,
    stat_send, stat_recv, dqs_send, dqs_recv, dqx_send, dqx_recv, a2a_send, a2a_recv,
):
    me = lax.axis_index("dp")
    my_owner = lax.axis_index("enc")
    n_pair = n_dp // 2
    pair, core = me // 2, me % 2
    sibling = pair * 2 + 1 - core
    rows, width = q_ref.shape
    passage_rows = p_ref.shape[0]
    blocks = passage_rows // BLOCK
    query_blocks = rows // BLOCK
    span_count = passage_rows // CH
    part = rows // CHUNKS
    slot_rows = CAP * CH

    def dp_target(index):
        return {"dp": index}

    barrier = pltpu.get_barrier_semaphore()
    for k in range(1, n_dp):
        pl.semaphore_signal(
            barrier, inc=1, device_id=dp_target((me + k) % n_dp),
            device_id_type=pl.DeviceIdType.MESH,
        )
    for k in range(1, n_enc):
        pl.semaphore_signal(
            barrier, inc=1, device_id={"enc": (my_owner + k) % n_enc},
            device_id_type=pl.DeviceIdType.MESH,
        )
    load_q = pltpu.make_async_copy(q_ref, q_all.at[rows_at(me, rows)], load_sem.at[0])
    load_p = pltpu.make_async_copy(p_ref, p_own, load_sem.at[1])
    load_q.start()
    load_p.start()
    pl.semaphore_wait(barrier, n_dp + n_enc - 2)

    def chunk(source, h):
        return pl.ds(pl.multiple_of(source * rows + h * part, part), part)

    def query_send(t, h):
        target = ((pair + t) % n_pair) * 2 + core
        return remote(
            q_ref.at[pl.ds(h * part, part)], q_all.at[chunk(me, h)],
            qx_send.at[t, h], qx_recv.at[t, h], dp_target(target),
        )

    def query_arrival(t, h):
        source = ((pair - t + n_pair) % n_pair) * 2 + core
        view = q_all.at[chunk(source, h)]
        return remote(view, view, qx_send.at[t, h], qx_recv.at[t, h], dp_target(source))

    def query_forward(t, h, owner_core):
        source = ((pair - t + n_pair) % n_pair) * 2 + owner_core
        view = q_all.at[chunk(source, h)]
        return remote(view, view, qf_send.at[t, h], qf_recv.at[t, h], dp_target(sibling))

    for h in range(CHUNKS):
        for t in range(1, n_pair):
            query_send(t, h).start()
    to_sibling = remote(
        q_ref, q_all.at[rows_at(me, rows)], qs_sem.at[0], qs_sem.at[1], dp_target(sibling)
    )
    to_sibling.start()

    code_out[...] = jnp.zeros_like(code_out)
    for b in range(query_blocks):
        for j in range(n_dp * blocks):
            hit = (positive_ref[0, b] == j).astype(jnp.int32)
            seen = (pattern_ref[0, b, j] == 1).astype(jnp.int32)
            value = jnp.maximum(2 * hit, seen).astype(jnp.float32)
            code_out[j // blocks, j % blocks : j % blocks + 1, b * BLOCK : (b + 1) * BLOCK] = (
                jnp.full((1, BLOCK), value, jnp.float32)
            )
    code_all[me] = code_out[me]

    def code_copy(k):
        target = (me + k) % n_dp
        return remote(
            code_out.at[target], code_all.at[me], code_send.at[k], code_recv.at[k],
            dp_target(target),
        )

    for k in range(1, n_dp):
        code_copy(k).start()

    def select_spans(owner, carry):
        seen = jnp.int32(0)
        found = [jnp.int32(-1)] * CAP
        for c in range(span_count):
            hit = (owners_ref[0, 0, c] == owner).astype(jnp.int32)
            for r in range(CAP):
                found[r] = found[r] + (c + 1) * hit * (seen == r).astype(jnp.int32)
            seen = seen + hit
        line = lax.broadcasted_iota(jnp.int32, (CH, passage_rows), 0)
        column = lax.broadcasted_iota(jnp.int32, (CH, passage_rows), 1)
        for r in range(CAP):
            chosen = (column == line + found[r] * CH).astype(jnp.float32)
            select[rows_at(owner * CAP + r, CH), :] = chosen.astype(jnp.bfloat16)
        return carry

    lax.fori_loop(0, n_enc, select_spans, 0)

    on_diagonal = (
        lax.broadcasted_iota(jnp.int32, (BLOCK, rows), 0)
        == lax.broadcasted_iota(jnp.int32, (BLOCK, rows), 1) % BLOCK
    )

    def score(source):
        columns = rows_at(source, rows)
        scores = lax.dot_general(
            p_own[...], q_all[columns, :], (((1,), (1,)), ((), ())),
            preferred_element_type=jnp.float32,
        ) * INVERSE_COOLNESS
        top = jnp.full((1, rows), NEVER, jnp.float32)
        picked = jnp.zeros((1, rows), jnp.float32)
        masked = []
        for j in range(blocks):
            block = scores[j * BLOCK : (j + 1) * BLOCK, :]
            code = code_all[source, j : j + 1, :]
            block_masked = jnp.where(code > 0.5, block, NEVER)
            masked.append(block_masked)
            top = jnp.maximum(top, jnp.max(block_masked, axis=0, keepdims=True))
            hit = on_diagonal & (code > 1.5)
            picked = picked + jnp.sum(jnp.where(hit, block, 0.0), axis=0, keepdims=True)
        shift = jnp.where(top > 0.5 * NEVER, top, 0.0)
        total = jnp.zeros((1, rows), jnp.float32)
        for j in range(blocks):
            terms = jnp.exp(masked[j] - shift)
            e_all[j * BLOCK : (j + 1) * BLOCK, columns] = terms
            total = total + jnp.sum(terms, axis=0, keepdims=True)
        top_all[0:1, columns] = top
        stat_all[me, 0:1, columns] = jnp.where(
            total > 0.0, shift + jnp.log(jnp.maximum(total, 1e-30)), NEVER
        )
        stat_all[me, 1:2, columns] = picked

    load_q.wait()
    load_p.wait()

    def code_wait(k):
        source = (me - k + n_dp) % n_dp
        remote(
            code_out.at[0], code_all.at[source], code_send.at[k], code_recv.at[k],
            dp_target(source),
        ).wait_recv()

    score(me)
    remote(
        q_ref, q_all.at[rows_at(sibling, rows)], qs_sem.at[0], qs_sem.at[1], dp_target(sibling)
    ).wait_recv()
    for k in range(1, n_dp):
        code_wait(k)
    score(sibling)

    def take(t, carry):
        first = ((pair - t + n_pair) % n_pair) * 2
        for h in range(CHUNKS):
            query_arrival(t, h).wait_recv()
            query_forward(t, h, core).start()
        score(first + core)
        for h in range(CHUNKS):
            query_forward(t, h, 1 - core).wait_recv()
        score(first + 1 - core)
        return carry

    lax.fori_loop(1, n_pair, take, 0)

    def stat_copy(k, source, target):
        view = stat_all.at[source]
        return remote(view, view, stat_send.at[k], stat_recv.at[k], dp_target(target))

    for k in range(1, n_dp):
        stat_copy(k, me, (me + k) % n_dp).start()
    for k in range(1, n_dp):
        stat_copy(k, (me - k + n_dp) % n_dp, me).wait_recv()

    def adjust(source, carry):
        columns = rows_at(source, rows)
        parts = [stat_all[d, 0:1, columns] for d in range(n_dp)]
        top = functools.reduce(jnp.maximum, parts)
        total = functools.reduce(jnp.add, [jnp.exp(x - top) for x in parts])
        log_total = top + jnp.log(total)
        factor = jnp.exp(top_all[0:1, columns] - log_total)
        for j in range(blocks):
            lines = slice(j * BLOCK, (j + 1) * BLOCK)
            hit = on_diagonal & (code_all[source, j : j + 1, :] > 1.5)
            probability = e_all[lines, columns] * factor
            adj[lines, columns] = (probability - jnp.where(hit, 1.0, 0.0)).astype(jnp.bfloat16)
        return carry

    lax.fori_loop(0, n_dp, adjust, 0)

    def span_copy(k, owner, place):
        return remote(
            outgoing.at[rows_at(owner, slot_rows)], received_ref.at[rows_at(place, slot_rows)],
            a2a_send.at[k], a2a_recv.at[k], {"enc": owner},
        )

    depth = min(n_dp * rows, 1024)
    for n in range(width // LANES):
        lanes = slice(n * LANES, (n + 1) * LANES)
        if depth == n_dp * rows:
            total = jnp.dot(adj[...], q_all[:, lanes], preferred_element_type=jnp.float32)
        else:
            dp_sum[...] = jnp.zeros_like(dp_sum)

            def add_group(g, carry, lanes=lanes):
                inner = rows_at(g, depth)
                dp_sum[...] += jnp.dot(
                    adj[:, inner], q_all[inner, lanes], preferred_element_type=jnp.float32
                )
                return carry

            lax.fori_loop(0, n_dp * rows // depth, add_group, 0)
            total = dp_sum[...]
        grad = (total * INVERSE_COOLNESS).astype(jnp.bfloat16)
        outgoing[:, lanes] = jnp.dot(
            select[...], grad, preferred_element_type=jnp.float32
        ).astype(jnp.bfloat16)

    def send_spans(k, carry):
        span_copy(k, (my_owner + k) % n_enc, my_owner).start()
        return carry

    lax.fori_loop(1, n_enc, send_spans, 0)
    keep = pltpu.make_async_copy(
        outgoing.at[rows_at(my_owner, slot_rows)],
        received_ref.at[rows_at(my_owner, slot_rows)],
        load_sem.at[2],
    )
    keep.start()

    def partial(source):
        return lax.dot_general(
            adj[:, rows_at(source, rows)], p_own[...], (((0,), (0,)), ((), ())),
            preferred_element_type=jnp.float32,
        )

    def dqs_copy(t):
        return remote(
            dqs_out.at[t], dqs_in.at[t], dqs_send.at[t], dqs_recv.at[t], dp_target(sibling)
        )

    def dqx_copy(t):
        target = ((pair + t) % n_pair) * 2 + core
        return remote(
            dqx_out.at[t], dqx_in.at[t], dqx_send.at[t], dqx_recv.at[t], dp_target(target)
        )

    def sibling_share(t, carry):
        target = ((pair + t) % n_pair) * 2
        dqs_out[t] = partial(target + 1 - core).astype(jnp.bfloat16)
        dqs_copy(t).start()
        return carry

    def chip_share(t, carry):
        target = ((pair + t) % n_pair) * 2
        dq_own[...] = partial(target + core)
        dqs_copy(t).wait_recv()
        dqx_out[t] = (dq_own[...] + dqs_in[t].astype(jnp.float32)).astype(jnp.bfloat16)
        dqx_copy(t).start()
        return carry

    lax.fori_loop(1, n_pair, sibling_share, 0)
    lax.fori_loop(1, n_pair, chip_share, 0)
    sibling_share(0, 0)
    dq_own[...] = partial(me)
    dqs_copy(0).wait_recv()
    dq_own[...] += dqs_in[0].astype(jnp.float32)

    own = rows_at(me, rows)
    parts = [stat_all[d, 0:1, own] for d in range(n_dp)]
    top = functools.reduce(jnp.maximum, parts)
    total = functools.reduce(jnp.add, [jnp.exp(x - top) for x in parts])
    picked = functools.reduce(jnp.add, [stat_all[d, 1:2, own] for d in range(n_dp)])
    losses_ref[...] = top + jnp.log(total) - picked

    def add_chip(t, carry):
        dqx_copy(t).wait_recv()
        dq_own[...] += dqx_in[t].astype(jnp.float32)
        return carry

    lax.fori_loop(1, n_pair, add_chip, 0)
    dq_ref[...] = (dq_own[...] * INVERSE_COOLNESS).astype(jnp.bfloat16)

    to_sibling.wait_send()
    for t in range(1, n_pair):
        for h in range(CHUNKS):
            query_send(t, h).wait_send()
            query_forward(t, h, core).wait_send()
    for k in range(1, n_dp):
        code_copy(k).wait_send()
        stat_copy(k, me, (me + k) % n_dp).wait_send()
    for t in range(n_pair):
        dqs_copy(t).wait_send()
        if t:
            dqx_copy(t).wait_send()
    for k in range(1, n_enc):
        span_copy(k, (my_owner + k) % n_enc, my_owner).wait_send()
        source = (my_owner - k + n_enc) % n_enc
        span_copy(k, source, source).wait_recv()
    keep.wait()


def owner_kernel(
    received_ref, cache_ref, weight_ref, losses_in, dq_in,
    hidden_ref, grad_ref, losses_ref, dq_ref,
    received, cache, weight, hidden, grad, dq, losses, in_sem, out_sem,
):
    loads = [
        pltpu.make_async_copy(source, place, in_sem.at[i])
        for i, (source, place) in enumerate(
            [
                (received_ref, received),
                (cache_ref, cache),
                (weight_ref, weight),
                (dq_in, dq),
                (losses_in, losses),
            ]
        )
    ]
    for load in loads:
        load.start()
    loads[0].wait()
    loads[1].wait()
    stores = []

    def store(source, place, lines):
        copy = pltpu.make_async_copy(
            source.at[lines], place.at[lines], out_sem.at[len(stores)]
        )
        copy.start()
        stores.append(copy)

    for n in range(0, cache.shape[1], LANES):
        lines = pl.ds(n, LANES)
        grad[lines, :] = lax.dot_general(
            cache[:, lines], received[...], (((0,), (0,)), ((), ())),
            preferred_element_type=jnp.float32,
        )
        store(grad, grad_ref, lines)
    loads[3].wait()
    store(dq, dq_ref, pl.ds(0, dq.shape[0]))
    loads[4].wait()
    store(losses, losses_ref, pl.ds(0, 1))
    loads[2].wait()
    part = received.shape[0] // 2
    for n in range(2):
        lines = pl.ds(n * part, part)
        hidden[lines, :] = lax.dot_general(
            received[lines, :], weight[...], (((1,), (1,)), ((), ())),
            preferred_element_type=jnp.float32,
        ).astype(jnp.bfloat16)
        store(hidden, hidden_ref, lines)
    for copy in stores:
        copy.wait()


def body(n_dp, n_enc, queries, passages, pattern, positive, owners, encoder_cache, proj_weight):
    rows, width = queries.shape[1:]
    passage_rows = passages.shape[1]
    blocks = passage_rows // BLOCK
    code_rows = -(-blocks // 4) * 4
    n_pair = n_dp // 2
    total_rows = n_dp * rows
    slots = n_enc * CAP * CH
    bf16, f32 = jnp.bfloat16, jnp.float32
    dma = pltpu.SemaphoreType.DMA
    smem = pl.BlockSpec(memory_space=pltpu.SMEM)
    vmem = pl.BlockSpec(memory_space=pltpu.VMEM)
    hbm = pl.BlockSpec(memory_space=pl.ANY)
    losses, dq, received = pl.pallas_call(
        functools.partial(group_kernel, n_dp, n_enc),
        out_shape=(
            jax.ShapeDtypeStruct((1, rows), f32),
            jax.ShapeDtypeStruct((rows, width), bf16),
            jax.ShapeDtypeStruct((slots, width), bf16),
        ),
        in_specs=[hbm, hbm, smem, smem, smem],
        out_specs=(vmem, vmem, hbm),
        scratch_shapes=[
            pltpu.VMEM((total_rows, width), bf16),
            pltpu.VMEM((passage_rows, width), bf16),
            pltpu.VMEM((n_dp, code_rows, rows), f32),
            pltpu.VMEM((n_dp, code_rows, rows), f32),
            pltpu.VMEM((passage_rows, total_rows), f32),
            pltpu.VMEM((passage_rows, total_rows), bf16),
            pltpu.VMEM((n_dp, 2, total_rows), f32),
            pltpu.VMEM((passage_rows, LANES), f32),
            pltpu.VMEM((slots, width), bf16),
            pltpu.VMEM((n_pair, rows, width), bf16),
            pltpu.VMEM((n_pair, rows, width), bf16),
            pltpu.VMEM((rows, width), f32),
            pltpu.VMEM((n_pair, rows, width), bf16),
            pltpu.VMEM((n_pair, rows, width), bf16),
            pltpu.VMEM((slots, passage_rows), bf16),
            pltpu.VMEM((1, total_rows), f32),
            dma((3,)),
            dma((2,)),
            dma((n_pair, CHUNKS)),
            dma((n_pair, CHUNKS)),
            dma((n_pair, CHUNKS)),
            dma((n_pair, CHUNKS)),
            dma((n_dp,)),
            dma((n_dp,)),
            dma((n_dp,)),
            dma((n_dp,)),
            dma((n_pair,)),
            dma((n_pair,)),
            dma((n_pair,)),
            dma((n_pair,)),
            dma((n_enc,)),
            dma((n_enc,)),
        ],
        compiler_params=pltpu.CompilerParams(
            collective_id=0, has_side_effects=True, vmem_limit_bytes=56 * 1024 * 1024
        ),
        cost_estimate=pl.CostEstimate(
            flops=6 * total_rows * passage_rows * width,
            bytes_accessed=4 * slots * width,
            transcendentals=2 * total_rows * passage_rows,
        ),
    )(queries[0], passages[0], pattern, positive, owners.transpose(0, 2, 1))
    owned, width_in = encoder_cache.shape[1:]
    hidden_grad, weight_grad, losses, dq = pl.pallas_call(
        owner_kernel,
        out_shape=(
            jax.ShapeDtypeStruct((slots, width_in), bf16),
            jax.ShapeDtypeStruct((width_in, width), f32),
            jax.ShapeDtypeStruct((1, rows), f32),
            jax.ShapeDtypeStruct((rows, width), bf16),
        ),
        in_specs=[hbm] * 5,
        out_specs=(hbm,) * 4,
        scratch_shapes=[
            pltpu.VMEM((slots, width), bf16),
            pltpu.VMEM((owned, width_in), bf16),
            pltpu.VMEM((width_in, width), bf16),
            pltpu.VMEM((slots, width_in), bf16),
            pltpu.VMEM((width_in, width), f32),
            pltpu.VMEM((rows, width), bf16),
            pltpu.VMEM((1, rows), f32),
            dma((5,)),
            dma((width_in // LANES + 4,)),
        ],
        compiler_params=pltpu.CompilerParams(vmem_limit_bytes=56 * 1024 * 1024),
        cost_estimate=pl.CostEstimate(
            flops=4 * slots * width * width_in,
            bytes_accessed=4 * width * width_in + 8 * slots * width,
            transcendentals=0,
        ),
    )(received, encoder_cache[0], proj_weight, losses, dq)
    return (losses, dq[None], hidden_grad[None], weight_grad[None])


def solution(mesh):
    placed = (
        P("enc", "dp", None),
        P("enc", "dp", None),
        P("enc", "dp", None),
        P("enc", "dp"),
        P("enc", "dp", None),
        P("enc", "dp", None),
        P(),
    )
    return jax.shard_map(
        functools.partial(body, mesh.shape["dp"], mesh.shape["enc"]),
        mesh=mesh,
        in_specs=placed,
        out_specs=(
            P("enc", "dp"),
            P("enc", "dp", None),
            P("enc", "dp", None),
            P("enc", "dp", None),
        ),
        check_vma=False,
    )
```
